512 devices in a mesh: turn: 8 (over x, core), river: 16 (over z), bucket: 4 (over y).
Axes of the slice: x: 4, y: 4, z: 16, core: 2. Of those that a mesh axis runs over, the one named last changes fastest.
Arguments:
- reach_in: float32 [8, 32, 1326], P('turn', 'river'), may hold values from 0.05 to 1
- hand_live: int32 [8, 32, 1326], P('turn', 'river'), may hold values 0 or 1
- hand_rank: int32 [8, 32, 1326], P('turn', 'river'), may hold values from 0 to 4095
- hand_bucket: int32 [8, 32, 1326], P('turn', 'river'), may hold values from 0 to 8959, as said below
- strategy: bfloat16 [8960, 384], P(('river', 'bucket')), may hold values from 0.049804688 to 1
- line_acts: int32 [512, 4], P('bucket'), may hold values from 0 to 384
- line_kind: int32 [512], P('bucket'), may hold values from 0 to 2
- line_pot: float32 [512], P('bucket'), may hold values from 2 to 24
Outputs:
- river_value: float32 [8, 32, 32, 1326], P('turn', 'river', 'bucket')
- turn_value: float32 [8, 32, 1326], P('turn', 'bucket')
- flop_value: float32 [32, 1326], P('bucket')
The draws below stay inside these ranges and needn't reach their ends.
Inputs may be any that keep to these rules, and one draw needn't show every extreme that they name: `hand_bucket`: on every board at most 64 hands have buckets in one device's block of 8960 / (river times bucket devices) consecutive table rows, and exactly 64 in some blocks of every board.
All inputs are finite; a program needn't handle non-finite values. No bound on the sum of `hand_live` on one device may be relied on, other than what follows from the above.
Results may differ from the reference program's by a relative error of at most 0.0003.
Values may be sent and summed in bfloat16 or wider, within the bound.
No kernel may reach another device: no remote copies, remote signals or barrier semaphores. Data moves between devices by JAX's collectives and lax.ppermute only.
A program may use at most 64 MiB of HBM per device.

```python
import math
import jax
import jax.numpy as jnp
import numpy as np
from jax import lax

HANDS = 1326
BUCKETS = 8960
ACTS = 384
DEPTH = 4
OPTIONS = 2
REPLIES = 8
TURNS = 8
RIVERS = 32
LINES = 512
ENTRIES = 32
CAP = 64
N_RIVER = 16
N_BUCKET = 4


def draw_hand_bucket(key, part):
    key = jax.random.fold_in(key, 11)
    owners = N_RIVER * N_BUCKET
    shard_rows = BUCKETS // owners
    hot_owners = max(owners // 8, 1)
    rest_hands = HANDS - hot_owners * CAP
    base_count = rest_hands // (owners - hot_owners)
    extra_count = rest_hands % (owners - hot_owners)
    order_index = jnp.arange(owners)
    counts = jnp.where(order_index < hot_owners, CAP, base_count + (order_index - hot_owners < extra_count).astype(jnp.int32))
    bounds = jnp.cumsum(counts.astype(jnp.int32))

    def one_board(board_key):
        perm_key, owner_key, row_key = jax.random.split(board_key, 3)
        position = jax.random.permutation(perm_key, HANDS)
        slot_owner = jnp.sum((position[:, None] >= bounds[None, :]).astype(jnp.int32), axis=1)
        owner_index = jax.random.permutation(owner_key, owners)[slot_owner]
        local_row = jax.random.randint(row_key, (HANDS,), 0, shard_rows)
        return owner_index * shard_rows + local_row
    board_keys = jax.random.split(key, TURNS * RIVERS)
    return jax.vmap(one_board)(board_keys).reshape(TURNS, RIVERS, HANDS).astype(jnp.int32)


def plant(array, stream_key, low, largest):
    longest = array.shape.index(max(array.shape))
    spots = []
    for shift in (0, 1):
        where = [jax.random.randint(jax.random.fold_in(stream_key, axis), (), 0, length) for axis, length in enumerate(array.shape)]
        where[longest] = (where[longest] + shift) % array.shape[longest]
        spots.append(tuple(where))
    return array.at[spots[0]].set(low).at[spots[1]].set(largest)


def level_of(own_key, extent, shards, smallest, high):
    def one(dim, blocks):
        heights = jax.random.uniform(jax.random.fold_in(jax.random.fold_in(own_key, 6), dim), (blocks,), jnp.float32, smallest / len(shards), high / len(shards))
        return jnp.repeat(jnp.exp(heights), extent[dim] // blocks).reshape((-1,) + (1,) * (len(extent) - dim - 1))

    loudness = one(*shards[0])
    for cut in shards[1:]:
        loudness = loudness * one(*cut)
    return loudness


def setup_inputs(seed: int = 0) -> dict:
    splits = jax.random.split(jax.random.key(seed), 9)
    reach_in = jnp.clip(jnp.exp(math.log(1.0) - 2.9957323 * jax.random.uniform(splits[0], (TURNS, RIVERS, HANDS), jnp.float32) ** level_of(splits[0], (TURNS, RIVERS, HANDS), ((0, 8), (1, 16)), -0.2, 0.2)), 0.05, 1.0)
    hand_live = plant((jax.random.randint(splits[1], (TURNS, RIVERS, HANDS), 0, 5) < 4).astype(jnp.int32), jax.random.fold_in(splits[1], 1), 0, 1)
    hand_rank = plant(jax.random.randint(splits[2], (TURNS, RIVERS, HANDS), 0, 4096), jax.random.fold_in(splits[2], 1), 0, 4095).astype(jnp.int32)
    hand_bucket = draw_hand_bucket(jax.random.fold_in(splits[8], 71), 0)
    strategy = jnp.clip(0.049804688 + 0.9501953 * jax.random.uniform(splits[4], (BUCKETS, ACTS), jnp.float32) ** level_of(splits[4], (BUCKETS, ACTS), ((0, 64),), -0.2, 0.2), 0.049804688, 1.0).astype(jnp.bfloat16)
    line_acts = plant(jax.random.randint(splits[5], (LINES, DEPTH), 0, ACTS + 1), jax.random.fold_in(splits[5], 1), 0, ACTS).astype(jnp.int32)
    line_kind = plant(jax.random.randint(splits[6], (LINES,), 0, 3), jax.random.fold_in(splits[6], 1), 0, 2).astype(jnp.int32)
    line_pot = jnp.clip(2.0 + 22.0 * jax.random.uniform(splits[7], (LINES,), jnp.float32) ** level_of(splits[7], (LINES,), ((0, 4),), -0.2, 0.2), 2.0, 24.0)
    return dict(reach_in=reach_in, hand_live=hand_live, hand_rank=hand_rank, hand_bucket=hand_bucket, strategy=strategy, line_acts=line_acts, line_kind=line_kind, line_pot=line_pot)


def card_table(count):
    upper_card, lower_card = np.triu_indices(52, 1)
    return jnp.asarray(upper_card[:count].astype(np.int32)), jnp.asarray(lower_card[:count].astype(np.int32))


def pair_tables(rank_rows, live_rows, rank_cols, live_cols, upper_rows, lower_rows, upper_cols, lower_cols):
    clashes = (upper_rows[:, None] == upper_cols[None, :]) | (upper_rows[:, None] == lower_cols[None, :])
    clashes = clashes | (lower_rows[:, None] == upper_cols[None, :]) | (lower_rows[:, None] == lower_cols[None, :])
    usable = jnp.logical_not(clashes) & (live_rows[:, None] > 0) & (live_cols[None, :] > 0)
    contest = jnp.where(usable, jnp.sign(rank_rows[:, None] - rank_cols[None, :]), 0)
    return contest.astype(jnp.bfloat16), usable.astype(jnp.bfloat16)


def reference(reach_in, hand_live, hand_rank, hand_bucket, strategy, line_acts, line_kind, line_pot):
    upper_card, lower_card = card_table(HANDS)
    padded = jnp.concatenate([strategy.astype(jnp.float32), jnp.ones((BUCKETS, 1), jnp.float32)], axis=1)
    payoff_sign = jnp.where(line_kind == 1, 1.0, jnp.where(line_kind == 2, -1.0, 0.0)).astype(jnp.float32)
    showdown_line = line_kind == 0
    scale_line = line_pot / HANDS

    def board_value(inputs):
        reach_row, live_row, rank_row, bucket_row = inputs
        bucket_rows = padded[bucket_row]
        product = (reach_row * live_row.astype(jnp.float32))[:, None]
        for depth_index in range(DEPTH):
            product = product * jnp.take(bucket_rows, line_acts[:, depth_index], axis=1)
        reach_line = product.astype(jnp.bfloat16)
        contest, usable = pair_tables(rank_row, live_row, rank_row, live_row, upper_card, lower_card, upper_card, lower_card)
        showdown = jnp.dot(contest, reach_line, preferred_element_type=jnp.float32)
        folded = jnp.dot(usable, reach_line, preferred_element_type=jnp.float32)
        values = jnp.where(showdown_line[None, :], showdown, payoff_sign[None, :] * folded) * scale_line[None, :]
        best_value = jnp.max(jnp.sum(values.reshape(HANDS, ENTRIES, OPTIONS, REPLIES), axis=3), axis=2)
        return best_value.T

    board_inputs = (reach_in.reshape(-1, HANDS), hand_live.reshape(-1, HANDS), hand_rank.reshape(-1, HANDS), hand_bucket.reshape(-1, HANDS))
    river_value = lax.map(board_value, board_inputs).reshape(TURNS, RIVERS, ENTRIES, HANDS)
    turn_value = jnp.sum(river_value, axis=1) / RIVERS
    flop_value = jnp.sum(turn_value, axis=0) / TURNS
    return river_value, turn_value, flop_value
```

```python
import functools

import jax
import jax.numpy as jnp
import numpy as np
from jax import lax
from jax.experimental import pallas as pl
from jax.experimental.pallas import tpu as pltpu
from jax.sharding import PartitionSpec as P

OPTIONS = 2
REPLIES = 8
LANES = 128
CORES = 2
F32 = jnp.float32
BF16 = jnp.bfloat16


def no_clash_table(count, padded):
    upper, lower = np.triu_indices(52, 1)
    upper, lower = upper[:count], lower[:count]
    clash = (upper[:, None] == upper) | (upper[:, None] == lower)
    clash |= (lower[:, None] == upper) | (lower[:, None] == lower)
    table = np.zeros((padded, padded), np.float32)
    table[:count, :count] = ~clash
    return jnp.asarray(table, BF16)


def split_two(x):
    high = x.astype(BF16)
    return high, (x - high.astype(F32)).astype(BF16)


def split_three(x):
    high = x.astype(BF16)
    rest = x - high.astype(F32)
    middle = rest.astype(BF16)
    return high, middle, (rest - middle.astype(F32)).astype(BF16)


def dot_rows(a, b):
    return lax.dot_general(a, b, (((1,), (1,)), ((), ())), preferred_element_type=F32)


def line_sum_kernel(hand_count, rows_ref, acts_ref, kind_ref, pot_ref, sums_ref):
    blocks, rows, width = rows_ref.shape
    lines = acts_ref.shape[0]
    entries = lines // (OPTIONS * REPLIES)
    table = rows_ref[...].reshape(blocks * rows, width)
    column = lax.broadcasted_iota(jnp.int32, (lines, width), 1)
    product = None
    for depth in range(acts_ref.shape[1]):
        picks = (acts_ref[:, depth : depth + 1] == column).astype(F32).astype(BF16)
        looked = dot_rows(table, picks)
        present = dot_rows(jnp.ones((8, width), BF16), picks)
        looked = looked + (1.0 - present[0:1])
        product = looked if product is None else product * looked
    kind = kind_ref[...]
    scale = pot_ref[...] / hand_count
    sign = jnp.where(kind == 1, 1.0, jnp.where(kind == 2, -1.0, 0.0))
    weights = (jnp.where(kind == 0, scale, 0.0), sign * scale)
    line = lax.broadcasted_iota(jnp.int32, (lines, LANES), 0)
    lane = lax.broadcasted_iota(jnp.int32, (lines, LANES), 1)
    slot = ((line // REPLIES) % OPTIONS) * entries + line // (REPLIES * OPTIONS)
    group = OPTIONS * entries
    total = jnp.zeros((rows, LANES), F32)
    for kind_index, weight in enumerate(weights):
        pieces = split_three(product * weight)
        for block in range(blocks):
            target = slot + (block * 2 + kind_index) * group
            gather = (lane == target).astype(F32).astype(BF16)
            for piece in pieces:
                total += jnp.dot(
                    piece[block * rows : (block + 1) * rows],
                    gather,
                    preferred_element_type=F32,
                )
    sums_ref[...] = total


def board_kernel(
    shard_rows, half_rows, blocks, core_ref, mine_ref, other_ref, reach_ref, live_ref, rank_ref,
    rank_col_ref, bucket_ref, table_ref, river_ref, part_ref, sums_ref, index_ref, group_ref,
    reach_scratch, rank_scratch, show_ref, fold_ref, contest_ref,
):
    boards, hands = reach_ref.shape
    padded = table_ref.shape[0]
    wide = index_ref.shape[1]
    held = mine_ref.shape[0]
    slots = 2 * held
    core = core_ref[0, 0]

    for part, ref in enumerate((mine_ref, other_ref)):
        for start in range(0, held, LANES):
            high, low = split_two(ref[start : start + LANES, :].T)
            at = part * held + start
            sums_ref[0:LANES, at : at + LANES] = high
            sums_ref[LANES : 2 * LANES, at : at + LANES] = low

    bucket = bucket_ref[...].astype(F32)
    owner = jnp.floor((bucket + 0.5) * (1.0 / shard_rows))
    row = bucket - owner * shard_rows
    place = jnp.floor((owner + 0.5) * (1.0 / blocks))
    block = owner - place * blocks
    half = jnp.where(row >= half_rows, 1.0, 0.0)
    row = row - half * (shard_rows - half_rows)
    elsewhere = jnp.where(half == core.astype(F32), 0.0, 1.0)
    index = elsewhere * held + place * half_rows + row
    index_ref[...] = jnp.full(index_ref.shape, -1, jnp.int32)
    group_ref[...] = jnp.zeros(group_ref.shape, F32)
    reach_scratch[...] = jnp.zeros(reach_scratch.shape, F32)
    rank_scratch[...] = jnp.zeros(rank_scratch.shape, F32)
    index_ref[0:boards, 0:hands] = index.astype(jnp.int32)
    group_ref[0:boards, 0:hands] = block
    reach_scratch[0:boards, 0:hands] = reach_ref[...] * live_ref[...].astype(F32)
    rank_scratch[0:boards, 0:hands] = rank_ref[...].astype(F32)

    step = 2 * LANES
    columns = LANES // blocks
    half_columns = columns // 2

    for board in range(boards):

        def gather(turn, carry, board=board):
            start = pl.multiple_of(turn * step, step)
            lanes = pl.ds(start, step)
            index = index_ref[board : board + 1, lanes]
            position = lax.broadcasted_iota(jnp.int32, (slots, step), 0)
            marks = (position == index).astype(F32).astype(BF16)
            found = jnp.dot(sums_ref[...], marks, preferred_element_type=F32)
            found = found[0:LANES] + found[LANES : 2 * LANES]
            group = group_ref[board : board + 1, lanes]
            chosen = jnp.zeros((columns, step), F32)
            for which in range(blocks):
                chosen += jnp.where(
                    group == which, found[which * columns : (which + 1) * columns], 0.0
                )
            chosen = chosen * reach_scratch[board : board + 1, lanes]
            high, low = split_two(chosen)
            show_ref[board, 0:half_columns, lanes] = high[0:half_columns]
            show_ref[board, half_columns:columns, lanes] = low[0:half_columns]
            base = board * columns
            fold_ref[base : base + half_columns, lanes] = high[half_columns:columns]
            fold_ref[base + half_columns : base + columns, lanes] = low[half_columns:columns]
            return carry

        lax.fori_loop(0, wide // step, gather, 0)

    folded = jnp.dot(fold_ref[:, 0:padded], table_ref[...], preferred_element_type=F32)
    total = None
    for board in range(boards):

        def build(turn, carry, board=board):
            rows = pl.ds(pl.multiple_of(turn * LANES, LANES), LANES)
            rank_row = rank_scratch[board : board + 1, :]
            rank_col = rank_col_ref[rows, board : board + 1]
            order = jnp.clip(rank_row - rank_col, -1.0, 1.0)
            contest_ref[rows, :] = (order * table_ref[rows, :].astype(F32)).astype(BF16)
            return carry

        lax.fori_loop(0, padded // LANES, build, 0)
        shown = jnp.dot(show_ref[board, :, 0:padded], contest_ref[...], preferred_element_type=F32)
        base = board * columns
        value = shown[0:half_columns] + shown[half_columns:columns]
        value = value + (
            folded[base : base + half_columns] + folded[base + half_columns : base + columns]
        )
        entries = half_columns // OPTIONS
        best = jnp.maximum(value[0:entries], value[entries:half_columns])
        best = best[:, 0:hands] * live_ref[board : board + 1, :].astype(F32)
        river_ref[board] = best
        total = best if total is None else total + best
    part_ref[...] = total


def whole_vmem():
    return pl.BlockSpec(memory_space=pltpu.VMEM)


def local(reach_in, hand_live, hand_rank, hand_bucket, strategy, line_acts, line_kind, line_pot):
    turns_here, rivers_here, hands = reach_in.shape
    boards = turns_here * rivers_here
    shard_rows, width = strategy.shape
    lines = line_acts.shape[0]
    entries = lines // (OPTIONS * REPLIES)
    blocks = lax.axis_size("bucket")
    rivers = lax.axis_size("river")
    turns = lax.axis_size("turn")
    padded = -(-hands // LANES) * LANES
    wide = -(-hands // (2 * LANES)) * 2 * LANES
    half_rows = -(-shard_rows // (CORES * 8)) * 8
    core = lax.axis_index("turn") % CORES

    with jax.named_scope("share_rows"):
        part = lax.dynamic_slice_in_dim(
            strategy, core * (shard_rows - half_rows), half_rows, axis=0
        )
        rows = lax.all_to_all(
            jnp.broadcast_to(part[None], (blocks, half_rows, width)),
            "bucket",
            split_axis=0,
            concat_axis=0,
            tiled=True,
        )
    with jax.named_scope("line_sums"):
        sums = pl.pallas_call(
            functools.partial(line_sum_kernel, hands),
            out_shape=jax.ShapeDtypeStruct((half_rows, LANES), F32),
            in_specs=[whole_vmem()] * 4,
            out_specs=whole_vmem(),
            compiler_params=pltpu.CompilerParams(vmem_limit_bytes=32 * 2**20),
        )(rows, line_acts, line_kind.reshape(1, lines), line_pot.reshape(1, lines))
    with jax.named_scope("share_sums"):
        mine = lax.all_gather(sums, "river", axis=0, tiled=True)
        swap = [(device, device ^ 1) for device in range(turns)]
        other = lax.ppermute(mine, "turn", swap)
    with jax.named_scope("boards"):
        rank = hand_rank.reshape(boards, hands)
        rank_col = jnp.pad(rank.T.astype(F32), ((0, padded - hands), (0, 0)))
        slots = 2 * rivers * half_rows
        river, partial = pl.pallas_call(
            functools.partial(board_kernel, shard_rows, half_rows, blocks),
            out_shape=(
                jax.ShapeDtypeStruct((boards, entries, hands), F32),
                jax.ShapeDtypeStruct((entries, hands), F32),
            ),
            in_specs=[pl.BlockSpec(memory_space=pltpu.SMEM)] + [whole_vmem()] * 8,
            out_specs=(whole_vmem(), whole_vmem()),
            scratch_shapes=[
                pltpu.VMEM((2 * LANES, slots), BF16),
                pltpu.VMEM((8, wide), jnp.int32),
                pltpu.VMEM((8, wide), F32),
                pltpu.VMEM((8, wide), F32),
                pltpu.VMEM((8, padded), F32),
                pltpu.VMEM((boards, LANES // blocks, wide), BF16),
                pltpu.VMEM((boards * LANES // blocks, wide), BF16),
                pltpu.VMEM((padded, padded), BF16),
            ],
            compiler_params=pltpu.CompilerParams(vmem_limit_bytes=48 * 2**20),
        )(
            core.astype(jnp.int32).reshape(1, 1),
            mine,
            other,
            reach_in.reshape(boards, hands),
            hand_live.reshape(boards, hands),
            rank,
            rank_col,
            hand_bucket.reshape(boards, hands),
            no_clash_table(hands, padded),
        )
    river_value = river.reshape(turns_here, rivers_here, entries, hands)
    with jax.named_scope("means"):
        by_river = lax.all_gather(partial, "river", axis=0, tiled=False)
        turn_value = jnp.sum(by_river, axis=0) / (rivers * rivers_here)
        by_turn = lax.all_gather(turn_value, "turn", axis=0, tiled=False)
        flop_value = jnp.sum(by_turn, axis=0) / (turns * turns_here)
    return river_value, turn_value[None], flop_value


def solution(mesh):
    return jax.shard_map(
        local,
        mesh=mesh,
        in_specs=(
            P("turn", "river", None),
            P("turn", "river", None),
            P("turn", "river", None),
            P("turn", "river", None),
            P(("river", "bucket"), None),
            P("bucket", None),
            P("bucket"),
            P("bucket"),
        ),
        out_specs=(
            P("turn", "river", "bucket", None),
            P("turn", "bucket", None),
            P("bucket", None),
        ),
        check_vma=False,
    )
```

```python
import functools

import jax
import jax.numpy as jnp
import numpy as np
from jax import lax
from jax.experimental import pallas as pl
from jax.experimental.pallas import tpu as pltpu
from jax.sharding import PartitionSpec as P

OPTIONS = 2
REPLIES = 8
LANES = 128
CARDS = 52
CORES = 2
F32 = jnp.float32
BF16 = jnp.bfloat16
I16 = jnp.int16
POT_MOST = 24.0
POT_LEAST = 2.0
CHANCE_LEAST = 0.049804688
CODE_MOST = 32000.0
GATHER_STEP = 512


def card_table(count, padded):
    table = np.zeros((LANES, padded), np.float32)
    for cards in np.triu_indices(CARDS, 1):
        table[cards[:count], np.arange(count)] = 1.0
    return jnp.asarray(table, BF16)


def code_scale(floor, most):
    return CODE_MOST / np.log2(1.0 + most / floor)


def sum_code(hands, depth):
    most = REPLIES * POT_MOST / hands
    floor = POT_LEAST / hands * CHANCE_LEAST**depth
    return floor, code_scale(floor, most)


def encode(x, floor, scale):
    size = jnp.log(1.0 + jnp.abs(x) * (1.0 / floor)) * (scale / np.log(2.0))
    size = jnp.minimum(jnp.floor(size + 0.5), 32767.0)
    return jnp.where(x < 0, -size, size).astype(jnp.int32).astype(I16)


def decode(code, floor, scale):
    code = code.astype(jnp.int32).astype(F32)
    size = (jnp.exp(jnp.abs(code) * (np.log(2.0) / scale)) - 1.0) * floor
    return jnp.where(code < 0, -size, size)


def encode_rows(x, hands):
    most = jnp.maximum(jnp.max(jnp.abs(x), axis=1, keepdims=True), 1e-30)
    power = jnp.floor(jnp.log(most) * (1.0 / np.log(2.0)) + 1.0)
    code = jnp.floor(x * (jnp.exp(power * -np.log(2.0)) * CODE_MOST) + 0.5)
    lane = lax.broadcasted_iota(jnp.int32, x.shape, 1)
    return jnp.where(lane == hands, power, code).astype(jnp.int32).astype(I16)


def decode_rows(code, hands):
    code = code.astype(jnp.int32).astype(F32)
    step = jnp.exp(code[:, hands : hands + 1] * np.log(2.0)) * (1.0 / CODE_MOST)
    return code[:, 0:hands] * step


def split_two(x):
    high = x.astype(BF16)
    return high, (x - high.astype(F32)).astype(BF16)


def split_three(x):
    high = x.astype(BF16)
    rest = x - high.astype(F32)
    middle = rest.astype(BF16)
    return high, middle, (rest - middle.astype(F32)).astype(BF16)


def dot_rows(a, b):
    return lax.dot_general(a, b, (((1,), (1,)), ((), ())), preferred_element_type=F32)


def line_sum_kernel(hand_count, code, rows_ref, acts_ref, info_ref, sums_ref):
    blocks, rows, width = rows_ref.shape
    lines, depth = acts_ref.shape
    entries = lines // (OPTIONS * REPLIES)
    table = rows_ref[...].reshape(blocks * rows, width)
    column = lax.broadcasted_iota(jnp.int32, (lines, width), 1)
    ones = jnp.ones((8, width), BF16)
    product = None
    for step in range(depth):
        picks = (acts_ref[:, step : step + 1] == column).astype(F32).astype(BF16)
        looked = dot_rows(table, picks) + (1.0 - dot_rows(ones, picks)[0:1])
        product = looked if product is None else product * looked
    kind = info_ref[0:1, :]
    scale = info_ref[1:2, :] / hand_count
    sign = jnp.where(kind == 1.0, 1.0, jnp.where(kind == 2.0, -1.0, 0.0))
    weights = (jnp.where(kind == 0.0, scale, 0.0), sign * scale)
    line = lax.broadcasted_iota(jnp.int32, (lines, LANES), 0)
    lane = lax.broadcasted_iota(jnp.int32, (lines, LANES), 1)
    slot = ((line // REPLIES) % OPTIONS) * entries + line // (REPLIES * OPTIONS)
    group = OPTIONS * entries
    total = jnp.zeros((rows, LANES), F32)
    for kind_index, weight in enumerate(weights):
        pieces = split_three(product * weight)
        for block in range(blocks):
            target = slot + (block * 2 + kind_index) * group
            gather = (lane == target).astype(F32).astype(BF16)
            for piece in pieces:
                total += jnp.dot(
                    piece[block * rows : (block + 1) * rows],
                    gather,
                    preferred_element_type=F32,
                )
    codes = encode(total, *code)
    for copy in range(sums_ref.shape[0]):
        sums_ref[copy] = codes


def prepare_kernel(
    shard_rows, half_rows, blocks, held, core_ref, reach_ref, live_ref, rank_ref, bucket_ref,
    cards_ref, contest_ref, rows_ref, turned_ref,
):
    boards, hands = reach_ref.shape
    padded = cards_ref.shape[1]
    core = core_ref[0, 0].astype(F32)
    bucket = bucket_ref[...].astype(F32)
    owner = jnp.floor((bucket + 0.5) * (1.0 / shard_rows))
    row = bucket - owner * shard_rows
    place = jnp.floor((owner + 0.5) * (1.0 / blocks))
    half = jnp.where(row >= half_rows, 1.0, 0.0)
    row = row - half * (shard_rows - half_rows)
    elsewhere = jnp.where(half == core, 0.0, 1.0)
    rows_ref[...] = jnp.full(rows_ref.shape, -1.0, F32)
    rows_ref[0:boards, 0:hands] = elsewhere * held + place * half_rows + row
    rows_ref[boards : 2 * boards, 0:hands] = owner - place * blocks
    rows_ref[2 * boards : 3 * boards, :] = jnp.zeros((boards, rows_ref.shape[1]), F32)
    rows_ref[2 * boards : 3 * boards, 0:hands] = reach_ref[...] * live_ref[...].astype(F32)

    turned_ref[...] = jnp.zeros(turned_ref.shape, F32)
    turned_ref[0:boards, 0:hands] = rank_ref[...].astype(F32)
    rank_rows = turned_ref[0:8, :]
    for start in range(0, padded, LANES):
        ranks = turned_ref[:, start : start + LANES].T
        cards = cards_ref[:, start : start + LANES].astype(F32).T.astype(BF16)
        shared = jnp.dot(cards, cards_ref[...], preferred_element_type=F32)
        for board in range(boards):
            order = rank_rows[board : board + 1, :] - ranks[:, board : board + 1]
            contest = jnp.where(shared == 0.0, jnp.clip(order, -1.0, 1.0), 0.0)
            contest_ref[board, start : start + LANES, :] = contest.astype(BF16)


def board_kernel(
    blocks, in_code, mine_ref, other_ref, live_ref, rows_hbm, cards_hbm, contest_hbm, river_ref,
    part_ref, rows_ref, cards_ref, contest_ref, plain_ref, sums_ref, show_ref, fold_ref,
    total_ref, rows_sem, cards_sem, contest_sem,
):
    rows_copy = pltpu.make_async_copy(rows_hbm, rows_ref, rows_sem)
    cards_copy = pltpu.make_async_copy(cards_hbm, cards_ref, cards_sem)
    contest_copy = pltpu.make_async_copy(contest_hbm, contest_ref, contest_sem)
    rows_copy.start()
    cards_copy.start()
    contest_copy.start()
    boards, hands = live_ref.shape
    padded = cards_ref.shape[1]
    wide = rows_ref.shape[1]
    rivers, half_rows, _ = mine_ref.shape
    held = rivers * half_rows
    slots = 2 * held

    for part, ref in enumerate((mine_ref, other_ref)):
        for river in range(rivers):
            at = part * held + river * half_rows
            plain_ref[at : at + half_rows, :] = decode(ref[river], *in_code)
    for start in range(0, slots, LANES):
        high, low = split_two(plain_ref[start : start + LANES, :].T)
        sums_ref[0:LANES, start : start + LANES] = high
        sums_ref[LANES : 2 * LANES, start : start + LANES] = low

    rows_copy.wait()
    step = GATHER_STEP
    columns = LANES // blocks
    half_columns = columns // 2

    for board in range(boards):

        def gather(turn, carry, board=board):
            lanes = pl.ds(pl.multiple_of(turn * step, step), step)
            index = rows_ref[board : board + 1, lanes].astype(jnp.int32)
            group = rows_ref[boards + board : boards + board + 1, lanes]
            reach = rows_ref[2 * boards + board : 2 * boards + board + 1, lanes]
            position = lax.broadcasted_iota(jnp.int32, (slots, step), 0)
            marks = (position == index).astype(F32).astype(BF16)
            found = jnp.dot(sums_ref[...], marks, preferred_element_type=F32)
            found = found[0:LANES] + found[LANES : 2 * LANES]
            chosen = jnp.zeros((columns, step), F32)
            for which in range(blocks):
                chosen += jnp.where(
                    group == which, found[which * columns : (which + 1) * columns], 0.0
                )
            high, low = split_two(chosen * reach)
            show_ref[board, 0:half_columns, lanes] = high[0:half_columns]
            show_ref[board, half_columns:columns, lanes] = low[0:half_columns]
            base = board * columns
            fold_ref[base : base + half_columns, lanes] = high[half_columns:columns]
            fold_ref[base + half_columns : base + columns, lanes] = low[half_columns:columns]
            return carry

        lax.fori_loop(0, wide // step, gather, 0)

    cards_copy.wait()
    row = lax.broadcasted_iota(jnp.int32, cards_ref.shape, 0)
    cards = jnp.where(row == CARDS, 1.0, cards_ref[...].astype(F32)).astype(BF16)
    folds = fold_ref[:, 0:padded]
    held_by = dot_rows(folds, cards)
    lane = lax.broadcasted_iota(jnp.int32, held_by.shape, 1)
    held_by = jnp.where(lane == CARDS, held_by, -held_by)
    folded = folds.astype(F32)
    for piece in split_three(held_by):
        folded += jnp.dot(piece, cards, preferred_element_type=F32)
    contest_copy.wait()
    total = None
    for board in range(boards):
        shown = jnp.dot(
            show_ref[board, :, 0:padded], contest_ref[board], preferred_element_type=F32
        )
        base = board * columns
        value = shown[0:half_columns] + shown[half_columns:columns]
        value = value + (
            folded[base : base + half_columns] + folded[base + half_columns : base + columns]
        )
        entries = half_columns // OPTIONS
        best = jnp.maximum(value[0:entries], value[entries:half_columns])
        best = best[:, 0:hands] * live_ref[board : board + 1, :].astype(F32)
        river_ref[board] = best
        total = best if total is None else total + best
    total_ref[...] = jnp.zeros(total_ref.shape, F32)
    total_ref[:, 0:hands] = total
    codes = encode_rows(total_ref[...], hands)
    for copy in range(part_ref.shape[0]):
        part_ref[copy] = codes


def river_mean_kernel(share, codes_ref, mean_ref, part_ref, total_ref):
    hands = mean_ref.shape[1]
    total = decode_rows(codes_ref[0], hands)
    for river in range(1, codes_ref.shape[0]):
        total += decode_rows(codes_ref[river], hands)
    mean = total * share
    mean_ref[...] = mean
    total_ref[...] = jnp.zeros(total_ref.shape, F32)
    total_ref[:, 0:hands] = mean
    codes = encode_rows(total_ref[...], hands)
    for copy in range(part_ref.shape[0]):
        part_ref[copy] = codes


def turn_mean_kernel(share, codes_ref, mean_ref):
    hands = mean_ref.shape[1]
    total = decode_rows(codes_ref[0], hands)
    for turn in range(1, codes_ref.shape[0]):
        total += decode_rows(codes_ref[turn], hands)
    mean_ref[...] = total * share


def whole_vmem():
    return pl.BlockSpec(memory_space=pltpu.VMEM)


def local(reach_in, hand_live, hand_rank, hand_bucket, strategy, line_acts, line_kind, line_pot):
    turns_here, rivers_here, hands = reach_in.shape
    boards = turns_here * rivers_here
    shard_rows, width = strategy.shape
    lines = line_acts.shape[0]
    entries = lines // (OPTIONS * REPLIES)
    blocks = lax.axis_size("bucket")
    rivers = lax.axis_size("river")
    turns = lax.axis_size("turn")
    padded = -(-hands // LANES) * LANES
    wide = -(-hands // GATHER_STEP) * GATHER_STEP
    half_rows = -(-shard_rows // (CORES * 8)) * 8
    core = lax.axis_index("turn") % CORES

    with jax.named_scope("share_rows"):
        part = lax.dynamic_slice_in_dim(
            strategy, core * (shard_rows - half_rows), half_rows, axis=0
        )
        rows = lax.all_to_all(
            jnp.broadcast_to(part[None], (blocks, half_rows, width)),
            "bucket",
            split_axis=0,
            concat_axis=0,
            tiled=True,
        )
    in_code = sum_code(hands, line_acts.shape[1])
    info = jnp.stack([line_kind.astype(F32), line_pot])
    with jax.named_scope("line_sums"):
        sums = pl.pallas_call(
            functools.partial(line_sum_kernel, hands, in_code),
            out_shape=jax.ShapeDtypeStruct((rivers, half_rows, LANES), I16),
            in_specs=[whole_vmem()] * 3,
            out_specs=whole_vmem(),
            compiler_params=pltpu.CompilerParams(vmem_limit_bytes=16 * 2**20),
        )(rows, line_acts, info)
    cards = card_table(hands, padded)
    live = hand_live.reshape(boards, hands)
    with jax.named_scope("share_sums"):
        mine = lax.all_to_all(sums, "river", split_axis=0, concat_axis=0, tiled=True)
    with jax.named_scope("prepare"):
        contest, hand_rows = pl.pallas_call(
            functools.partial(prepare_kernel, shard_rows, half_rows, blocks, rivers * half_rows),
            out_shape=(
                jax.ShapeDtypeStruct((boards, padded, padded), BF16),
                jax.ShapeDtypeStruct((8, wide), F32),
            ),
            in_specs=[pl.BlockSpec(memory_space=pltpu.SMEM)] + [whole_vmem()] * 5,
            out_specs=(whole_vmem(), whole_vmem()),
            scratch_shapes=[pltpu.VMEM((LANES, padded), F32)],
            cost_estimate=pl.CostEstimate(
                flops=8 * boards * padded * padded,
                bytes_accessed=(boards + 1) * 2 * padded * padded,
                transcendentals=0,
            ),
            compiler_params=pltpu.CompilerParams(vmem_limit_bytes=24 * 2**20),
        )(
            core.astype(jnp.int32).reshape(1, 1),
            reach_in.reshape(boards, hands),
            live,
            hand_rank.reshape(boards, hands),
            hand_bucket.reshape(boards, hands),
            cards,
        )
    mine, hand_rows = lax.optimization_barrier((mine, hand_rows))
    with jax.named_scope("share_sums"):
        swap = [(device, device ^ 1) for device in range(turns)]
        other = lax.ppermute(mine, "turn", swap)
    with jax.named_scope("boards"):
        slots = 2 * rivers * half_rows
        river, partial = pl.pallas_call(
            functools.partial(board_kernel, blocks, in_code),
            out_shape=(
                jax.ShapeDtypeStruct((boards, entries, hands), F32),
                jax.ShapeDtypeStruct((rivers, entries, padded), I16),
            ),
            in_specs=[whole_vmem()] * 3 + [pl.BlockSpec(memory_space=pltpu.HBM)] * 3,
            out_specs=(whole_vmem(), whole_vmem()),
            scratch_shapes=[
                pltpu.VMEM(hand_rows.shape, F32),
                pltpu.VMEM(cards.shape, BF16),
                pltpu.VMEM(contest.shape, BF16),
                pltpu.VMEM((slots, LANES), F32),
                pltpu.VMEM((2 * LANES, slots), BF16),
                pltpu.VMEM((boards, LANES // blocks, wide), BF16),
                pltpu.VMEM((boards * LANES // blocks, wide), BF16),
                pltpu.VMEM((entries, padded), F32),
                pltpu.SemaphoreType.DMA(()),
                pltpu.SemaphoreType.DMA(()),
                pltpu.SemaphoreType.DMA(()),
            ],
            compiler_params=pltpu.CompilerParams(vmem_limit_bytes=60 * 2**20),
        )(mine, other, live, hand_rows, cards, contest)
    river_value = river.reshape(turns_here, rivers_here, entries, hands)
    with jax.named_scope("means"):
        by_river = lax.all_to_all(partial, "river", split_axis=0, concat_axis=0, tiled=True)
        turn_value, partial = pl.pallas_call(
            functools.partial(river_mean_kernel, 1.0 / (rivers * rivers_here)),
            out_shape=(
                jax.ShapeDtypeStruct((entries, hands), F32),
                jax.ShapeDtypeStruct((turns, entries, padded), I16),
            ),
            in_specs=[whole_vmem()],
            out_specs=(whole_vmem(), whole_vmem()),
            scratch_shapes=[pltpu.VMEM((entries, padded), F32)],
        )(by_river)
        by_turn = lax.all_to_all(partial, "turn", split_axis=0, concat_axis=0, tiled=True)
        flop_value = pl.pallas_call(
            functools.partial(turn_mean_kernel, 1.0 / (turns * turns_here)),
            out_shape=jax.ShapeDtypeStruct((entries, hands), F32),
            in_specs=[whole_vmem()],
            out_specs=whole_vmem(),
        )(by_turn)
    return river_value, turn_value[None], flop_value


def solution(mesh):
    return jax.shard_map(
        local,
        mesh=mesh,
        in_specs=(
            P("turn", "river", None),
            P("turn", "river", None),
            P("turn", "river", None),
            P("turn", "river", None),
            P(("river", "bucket"), None),
            P("bucket", None),
            P("bucket"),
            P("bucket"),
        ),
        out_specs=(
            P("turn", "river", "bucket", None),
            P("turn", "bucket", None),
            P("bucket", None),
        ),
        check_vma=False,
    )
```

```python
import functools

import jax
import jax.numpy as jnp
import numpy as np
from jax import lax
from jax.experimental import pallas as pl
from jax.experimental.pallas import tpu as pltpu
from jax.sharding import PartitionSpec as P

OPTIONS = 2
REPLIES = 8
LANES = 128
CARDS = 52
CORES = 2
CONTEST_PLACES = 8
SMALL = 8 * 2**20
F32 = jnp.float32
BF16 = jnp.bfloat16
I16 = jnp.int16
POT_MOST = 24.0
POT_LEAST = 2.0
CHANCE_LEAST = 0.049804688
CODE_MOST = 32000.0


def card_table(count, padded):
    table = np.zeros((LANES, padded), np.float32)
    for cards in np.triu_indices(CARDS, 1):
        table[cards[:count], np.arange(count)] = 1.0
    return jnp.asarray(table, BF16)


def code_scale(floor, most):
    return CODE_MOST / np.log2(1.0 + most / floor)


def sum_code(hands, depth):
    most = REPLIES * POT_MOST / hands
    floor = POT_LEAST / hands * CHANCE_LEAST**depth
    return floor, code_scale(floor, most)


def encode(x, floor, scale):
    size = jnp.log(1.0 + jnp.abs(x) * (1.0 / floor)) * (scale / np.log(2.0))
    size = jnp.minimum(jnp.floor(size + 0.5), 32767.0)
    return jnp.where(x < 0, -size, size).astype(jnp.int32).astype(I16)


def decode(code, floor, scale):
    code = code.astype(jnp.int32).astype(F32)
    size = (jnp.exp(jnp.abs(code) * (np.log(2.0) / scale)) - 1.0) * floor
    return jnp.where(code < 0, -size, size)


def encode_rows(x, hands):
    most = jnp.maximum(jnp.max(jnp.abs(x), axis=1, keepdims=True), 1e-30)
    power = jnp.floor(jnp.log(most) * (1.0 / np.log(2.0)) + 1.0)
    code = jnp.floor(x * (jnp.exp(power * -np.log(2.0)) * CODE_MOST) + 0.5)
    lane = lax.broadcasted_iota(jnp.int32, x.shape, 1)
    return jnp.where(lane == hands, power, code).astype(jnp.int32).astype(I16)


def sum_decoded(codes_ref, hands):
    total = None
    for index in range(codes_ref.shape[0]):
        code = codes_ref[index].astype(jnp.int32).astype(F32)
        step = jnp.exp(code[:, hands : hands + 1] * np.log(2.0)) * (1.0 / CODE_MOST)
        part = code * step
        total = part if total is None else total + part
    return total


def split_two(x):
    high = x.astype(BF16)
    return high, (x - high.astype(F32)).astype(BF16)


def split_three(x):
    high = x.astype(BF16)
    rest = x - high.astype(F32)
    middle = rest.astype(BF16)
    return high, middle, (rest - middle.astype(F32)).astype(BF16)


def dot_rows(a, b):
    return lax.dot_general(a, b, (((1,), (1,)), ((), ())), preferred_element_type=F32)


def line_sum_kernel(hand_count, code, rows_ref, acts_ref, info_ref, sums_ref):
    blocks, rows, width = rows_ref.shape
    lines, depth = acts_ref.shape
    entries = lines // (OPTIONS * REPLIES)
    table = [rows_ref[block].astype(F32) for block in range(blocks)]
    table = jnp.concatenate(table, axis=0).astype(BF16)
    column = lax.broadcasted_iota(jnp.int32, (lines, width), 1)
    ones = jnp.ones((8, width), BF16)
    product = None
    for step in range(depth):
        picks = (acts_ref[:, step : step + 1] == column).astype(F32).astype(BF16)
        looked = dot_rows(table, picks) + (1.0 - dot_rows(ones, picks)[0:1])
        product = looked if product is None else product * looked
    kind = info_ref[0:1, :]
    scale = info_ref[1:2, :] / hand_count
    sign = jnp.where(kind == 1.0, 1.0, jnp.where(kind == 2.0, -1.0, 0.0))
    weights = (jnp.where(kind == 0.0, scale, 0.0), sign * scale)
    line = lax.broadcasted_iota(jnp.int32, (lines, LANES), 0)
    lane = lax.broadcasted_iota(jnp.int32, (lines, LANES), 1)
    slot = ((line // REPLIES) % OPTIONS) * entries + line // (REPLIES * OPTIONS)
    group = OPTIONS * entries
    total = jnp.zeros((rows, LANES), F32)
    for kind_index, weight in enumerate(weights):
        pieces = split_two(product * weight)
        for block in range(blocks):
            target = slot + (block * 2 + kind_index) * group
            gather = (lane == target).astype(F32).astype(BF16)
            for piece in pieces:
                total += jnp.dot(
                    piece[block * rows : (block + 1) * rows],
                    gather,
                    preferred_element_type=F32,
                )
    codes = encode(total, *code)
    for copy in range(sums_ref.shape[0]):
        sums_ref[copy] = codes


def prepare_kernel(
    shard_rows, held_rows, blocks, rivers, core_ref, reach_hbm, live_hbm, rank_hbm, bucket_hbm,
    cards_hbm, contest_hbm, rows_ref, slots_ref, token_ref, cards_ref, reach_ref, live_ref, rank_ref,
    bucket_ref, index_ref, turned_ref, contest_ref, in_sems, sems,
):
    arrays = (reach_hbm, live_hbm, rank_hbm, bucket_hbm, cards_hbm)
    places = (reach_ref, live_ref, rank_ref, bucket_ref, cards_ref)
    copies = []
    for index, (array, place) in enumerate(zip(arrays, places)):
        copies.append(pltpu.make_async_copy(array, place, in_sems.at[index]))
        copies[-1].start()
    boards, hands = reach_ref.shape
    padded = cards_ref.shape[1]
    chunks = padded // LANES
    token_ref[...] = jnp.zeros(token_ref.shape, I16)
    for copy in copies:
        copy.wait()
    bucket = bucket_ref[...].astype(F32)
    owner = jnp.floor((bucket + 0.5) * (1.0 / shard_rows))
    row = bucket - owner * shard_rows
    place = jnp.floor((owner + 0.5) * (1.0 / blocks))
    half = jnp.where(row >= held_rows, 1.0, 0.0)
    row = row - half * (shard_rows - held_rows)
    elsewhere = jnp.where(half == core_ref[0, 0].astype(F32), 0.0, 1.0)
    index_ref[...] = jnp.zeros(index_ref.shape, F32)
    index_ref[:, 0:hands] = (elsewhere * rivers + place) * held_rows + row
    slots_ref[...] = jnp.zeros(slots_ref.shape, jnp.int32)
    for board in range(boards):
        for chunk in range(chunks):
            slot = index_ref[board : board + 1, chunk * LANES : (chunk + 1) * LANES]
            at = board * chunks + chunk
            slots_ref[at : at + 1, :] = slot.astype(jnp.int32)
    rows_ref[...] = jnp.zeros(rows_ref.shape, F32)
    rows_ref[0:boards, 0:hands] = owner - place * blocks
    live = live_ref[...].astype(F32)
    rows_ref[boards : 2 * boards, 0:hands] = reach_ref[...] * live
    rows_ref[2 * boards : 3 * boards, 0:hands] = live

    turned_ref[...] = jnp.zeros(turned_ref.shape, F32)
    turned_ref[0:boards, 0:hands] = rank_ref[...].astype(F32)
    rank_rows = turned_ref[0:8, :]
    copies = []
    for chunk in range(chunks):
        lines = pl.ds(chunk * LANES, LANES)
        ranks = turned_ref[:, lines].T
        cards = cards_ref[:, lines].astype(F32).T.astype(BF16)
        shared = jnp.dot(cards, cards_ref[...], preferred_element_type=F32)
        for board in range(boards):
            order = rank_rows[board : board + 1, :] - ranks[:, board : board + 1]
            contest = jnp.where(shared == 0.0, jnp.clip(order, -1.0, 1.0), 0.0)
            contest_ref[board, lines, :] = contest.astype(BF16)
        copy = pltpu.make_async_copy(
            contest_ref.at[:, lines, :], contest_hbm.at[0:boards, lines, :], sems.at[chunk]
        )
        copy.start()
        copies.append(copy)
    for copy in copies:
        copy.wait()


def board_kernel(
    blocks, in_code, mine_ref, other_ref, rows_ref, cards_ref, contest_hbm, slots_hbm, river_hbm,
    part_ref, contest_ref, slots_ref, plain_ref, found_ref, show_ref, fold_ref, river_ref,
    contest_sems, slots_sem, river_sems,
):
    boards, _, hands = river_ref.shape
    padded = cards_ref.shape[1]
    chunks = padded // LANES
    rivers, held_rows, _ = mine_ref.shape
    columns = LANES // blocks
    half = columns // 2
    entries = half // OPTIONS
    slots_copy = pltpu.make_async_copy(slots_hbm, slots_ref, slots_sem)
    slots_copy.start()
    contest_copies = []
    for board in range(boards):
        contest_copies.append(
            pltpu.make_async_copy(
                contest_hbm.at[board], contest_ref.at[board], contest_sems.at[board]
            )
        )
        contest_copies[board].start()

    for part, ref in enumerate((mine_ref, other_ref)):
        for river in range(rivers):
            at = (part * rivers + river) * held_rows
            plain_ref[at : at + held_rows, :] = decode(ref[river], *in_code)
    slots_copy.wait()

    for board in range(boards):

        def gather(chunk, carry, board=board):
            base = pl.multiple_of(chunk * LANES, LANES)
            for hand in range(LANES):
                slot = slots_ref[board * chunks + chunk, hand]
                found_ref[pl.ds(base + hand, 1), :] = plain_ref[pl.ds(slot, 1), :]
            return carry

        lax.fori_loop(0, chunks, gather, 0)

        for chunk in range(chunks):
            lanes = pl.ds(chunk * LANES, LANES)
            found = found_ref[lanes, :].T
            group = rows_ref[board : board + 1, lanes]
            reach = rows_ref[boards + board : boards + board + 1, lanes]
            chosen = jnp.zeros((columns, LANES), F32)
            for which in range(blocks):
                chosen += jnp.where(
                    group == which, found[which * columns : (which + 1) * columns], 0.0
                )
            high, low = split_two(chosen * reach)
            show_ref[board, 0:half, lanes] = high[0:half]
            show_ref[board, half:columns, lanes] = low[0:half]
            base = board * columns
            fold_ref[base : base + half, lanes] = high[half:columns]
            fold_ref[base + half : base + columns, lanes] = low[half:columns]

    row = lax.broadcasted_iota(jnp.int32, cards_ref.shape, 0)
    cards = jnp.where(row == CARDS, 1.0, cards_ref[...].astype(F32)).astype(BF16)
    folds = fold_ref[...]
    held_by = dot_rows(folds, cards)
    lane = lax.broadcasted_iota(jnp.int32, held_by.shape, 1)
    held_by = jnp.where(lane == CARDS, held_by, -held_by)
    folded = folds.astype(F32)
    for piece in split_three(held_by):
        folded += jnp.dot(piece, cards, preferred_element_type=F32)
    total = None
    river_copies = []
    for board in range(boards):
        contest_copies[board].wait()
        shown = jnp.dot(show_ref[board], contest_ref[board], preferred_element_type=F32)
        base = board * columns
        value = shown[0:half] + shown[half:columns]
        value = value + (folded[base : base + half] + folded[base + half : base + columns])
        best = jnp.maximum(value[0:entries], value[entries:half])
        best = best * rows_ref[2 * boards + board : 2 * boards + board + 1, :]
        river_ref[board] = best[:, 0:hands]
        river_copies.append(
            pltpu.make_async_copy(river_ref.at[board], river_hbm.at[board], river_sems.at[board])
        )
        river_copies[board].start()
        total = best if total is None else total + best
    codes = encode_rows(total, hands)
    for copy in range(part_ref.shape[0]):
        part_ref[copy] = codes
    for copy in river_copies:
        copy.wait()


def river_mean_kernel(share, codes_ref, mean_ref, part_ref):
    hands = mean_ref.shape[1]
    mean = sum_decoded(codes_ref, hands) * share
    mean_ref[...] = mean[:, 0:hands]
    lane = lax.broadcasted_iota(jnp.int32, mean.shape, 1)
    codes = encode_rows(jnp.where(lane < hands, mean, 0.0), hands)
    for copy in range(part_ref.shape[0]):
        part_ref[copy] = codes


def turn_mean_kernel(share, codes_ref, turn_ref, turn_out_ref, mean_ref):
    hands = mean_ref.shape[1]
    turn_out_ref[...] = turn_ref[...]
    mean_ref[...] = sum_decoded(codes_ref, hands)[:, 0:hands] * share


def follow_kernel(value_ref, token_ref, out_ref):
    del value_ref, token_ref, out_ref


def whole_vmem():
    return pl.BlockSpec(memory_space=pltpu.VMEM)


def local(reach_in, hand_live, hand_rank, hand_bucket, strategy, line_acts, line_kind, line_pot):
    turns_here, rivers_here, hands = reach_in.shape
    boards = turns_here * rivers_here
    shard_rows, width = strategy.shape
    lines = line_acts.shape[0]
    entries = lines // (OPTIONS * REPLIES)
    blocks = lax.axis_size("bucket")
    rivers = lax.axis_size("river")
    turns = lax.axis_size("turn")
    padded = -(-hands // LANES) * LANES
    held_rows = -(-shard_rows // (CORES * 8)) * 8
    core = lax.axis_index("turn") % CORES

    with jax.named_scope("share_rows"):
        first = core * (shard_rows - held_rows)
        part = lax.dynamic_slice_in_dim(strategy, first, held_rows, axis=0)
        rows = lax.all_to_all(
            jnp.broadcast_to(part[None], (blocks, held_rows, width)),
            "bucket",
            split_axis=0,
            concat_axis=0,
            tiled=True,
        )
    in_code = sum_code(hands, line_acts.shape[1])
    info = jnp.stack([line_kind.astype(F32), line_pot])
    with jax.named_scope("line_sums"):
        sums = pl.pallas_call(
            functools.partial(line_sum_kernel, hands, in_code),
            out_shape=jax.ShapeDtypeStruct((rivers, held_rows, LANES), I16),
            in_specs=[whole_vmem()] * 3,
            out_specs=whole_vmem(),
            compiler_params=pltpu.CompilerParams(vmem_limit_bytes=16 * 2**20),
        )(rows, line_acts, info)
    cards = card_table(hands, padded)
    live = hand_live.reshape(boards, hands)
    with jax.named_scope("share_sums"):
        mine = lax.all_to_all(sums, "river", split_axis=0, concat_axis=0, tiled=True)
    with jax.named_scope("prepare"):
        chunks = padded // LANES
        slot_shape = (-(-boards * chunks // 8) * 8, LANES)
        contest, hand_rows, slots, token, cards = pl.pallas_call(
            functools.partial(prepare_kernel, shard_rows, held_rows, blocks, rivers),
            out_shape=(
                jax.ShapeDtypeStruct((CONTEST_PLACES, padded, padded), BF16),
                jax.ShapeDtypeStruct((8, padded), F32),
                jax.ShapeDtypeStruct(slot_shape, jnp.int32),
                jax.ShapeDtypeStruct((16, LANES), I16),
                jax.ShapeDtypeStruct(cards.shape, BF16),
            ),
            in_specs=[pl.BlockSpec(memory_space=pltpu.SMEM)]
            + [pl.BlockSpec(memory_space=pl.ANY)] * 5,
            out_specs=(pl.BlockSpec(memory_space=pl.ANY),) + (whole_vmem(),) * 4,
            scratch_shapes=[
                pltpu.VMEM((boards, hands), F32),
                pltpu.VMEM((boards, hands), jnp.int32),
                pltpu.VMEM((boards, hands), jnp.int32),
                pltpu.VMEM((boards, hands), jnp.int32),
                pltpu.VMEM((boards, padded), F32),
                pltpu.VMEM((LANES, padded), F32),
                pltpu.VMEM((boards, padded, padded), BF16),
                pltpu.SemaphoreType.DMA((5,)),
                pltpu.SemaphoreType.DMA((chunks,)),
            ],
            cost_estimate=pl.CostEstimate(
                flops=8 * boards * padded * padded,
                bytes_accessed=(boards + 1) * 2 * padded * padded,
                transcendentals=0,
            ),
            compiler_params=pltpu.CompilerParams(vmem_limit_bytes=40 * 2**20),
        )(
            core.astype(jnp.int32).reshape(1, 1),
            reach_in.reshape(boards, hands),
            live,
            hand_rank.reshape(boards, hands),
            hand_bucket.reshape(boards, hands),
            cards,
        )
    with jax.named_scope("share_sums"):
        mine = pl.pallas_call(
            follow_kernel,
            out_shape=jax.ShapeDtypeStruct(mine.shape, mine.dtype),
            in_specs=[whole_vmem()] * 2,
            out_specs=whole_vmem(),
            input_output_aliases={0: 0},
            compiler_params=pltpu.CompilerParams(vmem_limit_bytes=SMALL),
        )(mine, token)
        swap = [(device, device ^ 1) for device in range(turns)]
        other = lax.ppermute(mine, "turn", swap)
    with jax.named_scope("boards"):
        river, partial = pl.pallas_call(
            functools.partial(board_kernel, blocks, in_code),
            out_shape=(
                jax.ShapeDtypeStruct((boards, entries, hands), F32),
                jax.ShapeDtypeStruct((rivers, entries, padded), I16),
            ),
            in_specs=[whole_vmem()] * 4 + [pl.BlockSpec(memory_space=pl.ANY)] * 2,
            out_specs=(pl.BlockSpec(memory_space=pl.ANY), whole_vmem()),
            scratch_shapes=[
                pltpu.VMEM((boards, padded, padded), BF16),
                pltpu.SMEM(slots.shape, jnp.int32),
                pltpu.VMEM((CORES * rivers * held_rows, LANES), F32),
                pltpu.VMEM((padded, LANES), F32),
                pltpu.VMEM((boards, LANES // blocks, padded), BF16),
                pltpu.VMEM((boards * LANES // blocks, padded), BF16),
                pltpu.VMEM((boards, entries, hands), F32),
                pltpu.SemaphoreType.DMA((boards,)),
                pltpu.SemaphoreType.DMA(()),
                pltpu.SemaphoreType.DMA((boards,)),
            ],
            compiler_params=pltpu.CompilerParams(vmem_limit_bytes=40 * 2**20),
        )(mine, other, hand_rows, cards, contest, slots)
    with jax.named_scope("means"):
        by_river = lax.all_to_all(partial, "river", split_axis=0, concat_axis=0, tiled=True)
        turn_value, partial = pl.pallas_call(
            functools.partial(river_mean_kernel, 1.0 / (rivers * rivers_here)),
            out_shape=(
                jax.ShapeDtypeStruct((entries, hands), F32),
                jax.ShapeDtypeStruct((turns, entries, padded), I16),
            ),
            in_specs=[whole_vmem()],
            out_specs=(whole_vmem(), whole_vmem()),
            compiler_params=pltpu.CompilerParams(vmem_limit_bytes=SMALL),
        )(by_river)
        by_turn = lax.all_to_all(partial, "turn", split_axis=0, concat_axis=0, tiled=True)
        turn_value, flop_value = pl.pallas_call(
            functools.partial(turn_mean_kernel, 1.0 / (turns * turns_here)),
            out_shape=(
                jax.ShapeDtypeStruct(turn_value.shape, F32),
                jax.ShapeDtypeStruct((entries, hands), F32),
            ),
            in_specs=[whole_vmem()] * 2,
            out_specs=(whole_vmem(), whole_vmem()),
            compiler_params=pltpu.CompilerParams(vmem_limit_bytes=SMALL),
        )(by_turn, turn_value)
    river_value = river.reshape(turns_here, rivers_here, entries, hands)
    return river_value, turn_value[None], flop_value


def solution(mesh):
    return jax.shard_map(
        local,
        mesh=mesh,
        in_specs=(
            P("turn", "river", None),
            P("turn", "river", None),
            P("turn", "river", None),
            P("turn", "river", None),
            P(("river", "bucket"), None),
            P("bucket", None),
            P("bucket"),
            P("bucket"),
        ),
        out_specs=(
            P("turn", "river", "bucket", None),
            P("turn", "bucket", None),
            P("bucket", None),
        ),
        check_vma=False,
    )
```

```python
import functools

import jax
import jax.numpy as jnp
import numpy as np
from jax import lax
from jax.experimental import pallas as pl
from jax.experimental.pallas import tpu as pltpu
from jax.sharding import PartitionSpec as P

OPTIONS = 2
REPLIES = 8
LANES = 128
CARDS = 52
TILE = 16
CORES = 2
CONTEST_PLACES = 8
SMALL = 8 * 2**20
F32 = jnp.float32
BF16 = jnp.bfloat16
I16 = jnp.int16
POT_MOST = 24.0
POT_LEAST = 2.0
CHANCE_LEAST = 0.049804688
CODE_MOST = 32000.0


def card_table(count, padded):
    table = np.zeros((LANES, padded), np.float32)
    for cards in np.triu_indices(CARDS, 1):
        table[cards[:count], np.arange(count)] = 1.0
    return jnp.asarray(table, BF16)


def code_scale(floor, most):
    return CODE_MOST / np.log2(1.0 + most / floor)


def sum_code(hands, depth):
    most = REPLIES * POT_MOST / hands
    floor = POT_LEAST / hands * CHANCE_LEAST**depth
    return floor, code_scale(floor, most)


def encode(x, floor, scale):
    size = jnp.log(1.0 + jnp.abs(x) * (1.0 / floor)) * (scale / np.log(2.0))
    size = jnp.minimum(jnp.floor(size + 0.5), 32767.0)
    return jnp.where(x < 0, -size, size).astype(jnp.int32).astype(I16)


def decode(code, floor, scale):
    code = code.astype(jnp.int32).astype(F32)
    size = (jnp.exp(jnp.abs(code) * (np.log(2.0) / scale)) - 1.0) * floor
    return jnp.where(code < 0, -size, size)


def encode_rows(x, hands):
    most = jnp.maximum(jnp.max(jnp.abs(x), axis=1, keepdims=True), 1e-30)
    power = jnp.floor(jnp.log(most) * (1.0 / np.log(2.0)) + 1.0)
    code = jnp.floor(x * (jnp.exp(power * -np.log(2.0)) * CODE_MOST) + 0.5)
    lane = lax.broadcasted_iota(jnp.int32, x.shape, 1)
    return jnp.where(lane == hands, power, code).astype(jnp.int32).astype(I16)


def sum_decoded(codes_ref, hands):
    total = None
    for index in range(codes_ref.shape[0]):
        code = codes_ref[index].astype(jnp.int32).astype(F32)
        step = jnp.exp(code[:, hands : hands + 1] * np.log(2.0)) * (1.0 / CODE_MOST)
        part = code * step
        total = part if total is None else total + part
    return total


def split_two(x):
    high = x.astype(BF16)
    return high, (x - high.astype(F32)).astype(BF16)


def split_three(x):
    high = x.astype(BF16)
    rest = x - high.astype(F32)
    middle = rest.astype(BF16)
    return high, middle, (rest - middle.astype(F32)).astype(BF16)


def dot_rows(a, b):
    return lax.dot_general(a, b, (((1,), (1,)), ((), ())), preferred_element_type=F32)


def line_sum_kernel(hand_count, code, rows_ref, info_ref, sums_ref):
    blocks, rows, width = rows_ref.shape
    depth, lines = info_ref.shape
    depth -= 2
    entries = lines // (OPTIONS * REPLIES)
    table = [rows_ref[block].astype(F32) for block in range(blocks)]
    table = jnp.concatenate(table, axis=0).astype(BF16)
    column = lax.broadcasted_iota(jnp.int32, (width, lines), 0).astype(F32)
    picks = [
        (column == info_ref[step : step + 1, :]).astype(F32).astype(BF16) for step in range(depth)
    ]
    picks = jnp.concatenate(picks, axis=1)
    present = jnp.dot(jnp.ones((8, width), BF16), picks, preferred_element_type=F32)
    looked = jnp.dot(table, picks, preferred_element_type=F32) + (1.0 - present[0:1])
    product = looked[:, 0:lines]
    for step in range(1, depth):
        product = product * looked[:, step * lines : (step + 1) * lines]
    kind = info_ref[depth : depth + 1, :]
    scale = info_ref[depth + 1 : depth + 2, :] / hand_count
    sign = jnp.where(kind == 1.0, 1.0, jnp.where(kind == 2.0, -1.0, 0.0))
    weights = (jnp.where(kind == 0.0, scale, 0.0), sign * scale)
    line = lax.broadcasted_iota(jnp.int32, (lines, LANES), 0)
    lane = lax.broadcasted_iota(jnp.int32, (lines, LANES), 1)
    slot = ((line // REPLIES) % OPTIONS) * entries + line // (REPLIES * OPTIONS)
    group = OPTIONS * entries
    terms, targets = [], []
    for kind_index, weight in enumerate(weights):
        terms.extend(split_three(product * weight))
        targets.extend([(lane == slot + kind_index * group).astype(F32).astype(BF16)] * 3)
    summed = jnp.dot(
        jnp.concatenate(terms, axis=1),
        jnp.concatenate(targets, axis=0),
        preferred_element_type=F32,
    )
    total = summed[0:rows]
    for block in range(1, blocks):
        part = summed[block * rows : (block + 1) * rows]
        total += pltpu.roll(part, block * 2 * group, 1)
    codes = encode(total, *code)
    for copy in range(sums_ref.shape[0]):
        sums_ref[copy] = codes


def prepare_kernel(
    shard_rows, held_rows, blocks, rivers, reach_hbm, live_hbm, rank_hbm, bucket_hbm,
    cards_hbm, contest_hbm, rows_ref, slots_ref, token_ref, cards_ref, reach_ref, live_ref, rank_ref,
    bucket_ref, index_ref, turned_ref, contest_ref, in_sems, sems,
):
    arrays = (reach_hbm, live_hbm, rank_hbm, bucket_hbm, cards_hbm)
    places = (reach_ref, live_ref, rank_ref, bucket_ref, cards_ref)
    copies = []
    for index, (array, place) in enumerate(zip(arrays, places)):
        copies.append(pltpu.make_async_copy(array, place, in_sems.at[index]))
        copies[-1].start()
    boards, hands = reach_ref.shape
    padded = cards_ref.shape[1]
    chunks = padded // LANES
    token_ref[...] = jnp.zeros(token_ref.shape, I16)
    for copy in copies:
        copy.wait()
    bucket = bucket_ref[...].astype(F32)
    owner = jnp.floor((bucket + 0.5) * (1.0 / shard_rows))
    row = bucket - owner * shard_rows
    place = jnp.floor((owner + 0.5) * (1.0 / blocks))
    half = jnp.where(row >= held_rows, 1.0, 0.0)
    row = row - half * (shard_rows - held_rows)
    core = lax.rem(lax.axis_index("turn"), CORES).astype(F32)
    elsewhere = jnp.where(half == core, 0.0, 1.0)
    index_ref[...] = jnp.zeros(index_ref.shape, F32)
    index_ref[:, 0:hands] = (elsewhere * rivers + place) * held_rows + row
    slots_ref[...] = jnp.zeros(slots_ref.shape, jnp.int32)
    for board in range(boards):
        for chunk in range(chunks):
            slot = index_ref[board : board + 1, chunk * LANES : (chunk + 1) * LANES]
            at = board * chunks + chunk
            slots_ref[at : at + 1, :] = slot.astype(jnp.int32)
    rows_ref[...] = jnp.zeros(rows_ref.shape, F32)
    rows_ref[0:boards, 0:hands] = owner - place * blocks
    live = live_ref[...].astype(F32)
    rows_ref[boards : 2 * boards, 0:hands] = reach_ref[...] * live
    rows_ref[2 * boards : 3 * boards, 0:hands] = live

    turned_ref[...] = jnp.zeros(turned_ref.shape, F32)
    turned_ref[0:boards, 0:hands] = rank_ref[...].astype(F32)
    rank_rows = turned_ref[0:8, :]
    copies = []
    for chunk in range(chunks):
        lines = pl.ds(chunk * LANES, LANES)
        ranks = turned_ref[:, lines].T
        cards = cards_ref[:, lines].astype(F32).T.astype(BF16)
        shared = jnp.dot(cards, cards_ref[...], preferred_element_type=F32)
        for board in range(boards):
            order = rank_rows[board : board + 1, :] - ranks[:, board : board + 1]
            contest = jnp.where(shared == 0.0, jnp.clip(order, -1.0, 1.0), 0.0)
            contest_ref[board, lines, :] = contest.astype(BF16)
        copy = pltpu.make_async_copy(
            contest_ref.at[:, lines, :], contest_hbm.at[0:boards, lines, :], sems.at[chunk]
        )
        copy.start()
        copies.append(copy)
    around = cards_ref[TILE * (CARDS // TILE) : TILE * (CARDS // TILE + 1), :].astype(F32)
    row = lax.broadcasted_iota(jnp.int32, around.shape, 0)
    around = jnp.where(row == CARDS % TILE, 1.0, around).astype(BF16)
    cards_ref[TILE * (CARDS // TILE) : TILE * (CARDS // TILE + 1), :] = around
    for copy in copies:
        copy.wait()


def board_kernel(
    blocks, in_code, mine_ref, other_ref, rows_ref, cards_ref, contest_hbm, slots_hbm, river_hbm,
    part_ref, contest_ref, slots_ref, plain_ref, found_ref, show_ref, fold_ref, river_ref,
    contest_sems, slots_sem, river_sems,
):
    boards, _, hands = river_ref.shape
    padded = cards_ref.shape[1]
    chunks = padded // LANES
    rivers, held_rows, _ = mine_ref.shape
    columns = LANES // blocks
    half = columns // 2
    entries = half // OPTIONS
    slots_copy = pltpu.make_async_copy(slots_hbm, slots_ref, slots_sem)
    slots_copy.start()
    contest_copies = []
    for board in range(boards):
        contest_copies.append(
            pltpu.make_async_copy(
                contest_hbm.at[board], contest_ref.at[board], contest_sems.at[board]
            )
        )
        contest_copies[board].start()

    for part, ref in enumerate((mine_ref, other_ref)):
        for river in range(rivers):
            at = (part * rivers + river) * held_rows
            plain_ref[at : at + held_rows, :] = decode(ref[river], *in_code)
    slots_copy.wait()

    for board in range(boards):

        def gather(chunk, carry, board=board):
            base = pl.multiple_of(chunk * LANES, LANES)
            for hand in range(LANES):
                slot = slots_ref[board * chunks + chunk, hand]
                found_ref[pl.ds(base + hand, 1), :] = plain_ref[pl.ds(slot, 1), :]
            return carry

        lax.fori_loop(0, chunks, gather, 0)

        for chunk in range(chunks):
            lanes = pl.ds(chunk * LANES, LANES)
            found = found_ref[lanes, :].T
            group = rows_ref[board : board + 1, lanes]
            reach = rows_ref[boards + board : boards + board + 1, lanes]
            chosen = jnp.zeros((columns, LANES), F32)
            for which in range(blocks):
                chosen += jnp.where(
                    group == which, found[which * columns : (which + 1) * columns], 0.0
                )
            high, low = split_two(chosen * reach)
            show_ref[board, 0:half, lanes] = high[0:half]
            show_ref[board, half:columns, lanes] = low[0:half]
            base = board * half
            fold_ref[base : base + half, lanes] = high[half:columns]
            base = (boards + board) * half
            fold_ref[base : base + half, lanes] = low[half:columns]

    cards = cards_ref[...]
    folds = fold_ref[...]
    held_by = dot_rows(folds, cards)
    held_by = held_by[0 : boards * half] + held_by[boards * half : 2 * boards * half]
    lane = lax.broadcasted_iota(jnp.int32, held_by.shape, 1)
    held_by = jnp.where(lane == CARDS, held_by, -held_by)
    spread = jnp.dot(
        jnp.concatenate(split_three(held_by), axis=0), cards, preferred_element_type=F32
    )
    folded = folds[0 : boards * half].astype(F32) + folds[boards * half :].astype(F32)
    for piece in range(3):
        folded += spread[piece * boards * half : (piece + 1) * boards * half]
    total = None
    river_copies = []
    for board in range(boards):
        contest_copies[board].wait()
        shown = jnp.dot(show_ref[board], contest_ref[board], preferred_element_type=F32)
        value = shown[0:half] + shown[half:columns] + folded[board * half : (board + 1) * half]
        best = jnp.maximum(value[0:entries], value[entries:half])
        best = best * rows_ref[2 * boards + board : 2 * boards + board + 1, :]
        river_ref[board] = best[:, 0:hands]
        river_copies.append(
            pltpu.make_async_copy(river_ref.at[board], river_hbm.at[board], river_sems.at[board])
        )
        river_copies[board].start()
        total = best if total is None else total + best
    codes = encode_rows(total, hands)
    for copy in range(part_ref.shape[0]):
        part_ref[copy] = codes
    for copy in river_copies:
        copy.wait()


def river_mean_kernel(share, codes_ref, mean_ref, part_ref):
    hands = mean_ref.shape[1]
    mean = sum_decoded(codes_ref, hands) * share
    mean_ref[...] = mean[:, 0:hands]
    lane = lax.broadcasted_iota(jnp.int32, mean.shape, 1)
    codes = encode_rows(jnp.where(lane < hands, mean, 0.0), hands)
    for copy in range(part_ref.shape[0]):
        part_ref[copy] = codes


def turn_mean_kernel(share, codes_ref, turn_ref, turn_out_ref, mean_ref):
    hands = mean_ref.shape[1]
    turn_out_ref[...] = turn_ref[...]
    mean_ref[...] = sum_decoded(codes_ref, hands)[:, 0:hands] * share


def follow_kernel(value_ref, token_ref, out_ref):
    del value_ref, token_ref, out_ref


def whole_vmem():
    return pl.BlockSpec(memory_space=pltpu.VMEM)


def local(reach_in, hand_live, hand_rank, hand_bucket, strategy, line_acts, line_kind, line_pot):
    turns_here, rivers_here, hands = reach_in.shape
    boards = turns_here * rivers_here
    shard_rows, width = strategy.shape
    lines = line_acts.shape[0]
    entries = lines // (OPTIONS * REPLIES)
    blocks = lax.axis_size("bucket")
    rivers = lax.axis_size("river")
    turns = lax.axis_size("turn")
    padded = -(-hands // LANES) * LANES
    held_rows = -(-shard_rows // (CORES * 8)) * 8
    core = lax.axis_index("turn") % CORES

    with jax.named_scope("share_rows"):
        first = core * (shard_rows - held_rows)
        part = lax.dynamic_slice_in_dim(strategy, first, held_rows, axis=0)
        rows = lax.all_to_all(
            jnp.broadcast_to(part[None], (blocks, held_rows, width)),
            "bucket",
            split_axis=0,
            concat_axis=0,
            tiled=True,
        )
    in_code = sum_code(hands, line_acts.shape[1])
    info = [line_acts.T.astype(F32), line_kind.astype(F32)[None], line_pot[None]]
    info = jnp.concatenate(info, axis=0)
    with jax.named_scope("line_sums"):
        sums = pl.pallas_call(
            functools.partial(line_sum_kernel, hands, in_code),
            out_shape=jax.ShapeDtypeStruct((rivers, held_rows, LANES), I16),
            in_specs=[whole_vmem()] * 2,
            out_specs=whole_vmem(),
            compiler_params=pltpu.CompilerParams(vmem_limit_bytes=16 * 2**20),
        )(rows, info)
    cards = card_table(hands, padded)
    live = hand_live.reshape(boards, hands)
    with jax.named_scope("share_sums"):
        mine = lax.all_to_all(sums, "river", split_axis=0, concat_axis=0, tiled=True)
    with jax.named_scope("prepare"):
        chunks = padded // LANES
        slot_shape = (-(-boards * chunks // 8) * 8, LANES)
        contest, hand_rows, slots, token, cards = pl.pallas_call(
            functools.partial(prepare_kernel, shard_rows, held_rows, blocks, rivers),
            out_shape=(
                jax.ShapeDtypeStruct((CONTEST_PLACES, padded, padded), BF16),
                jax.ShapeDtypeStruct((8, padded), F32),
                jax.ShapeDtypeStruct(slot_shape, jnp.int32),
                jax.ShapeDtypeStruct((16, LANES), I16),
                jax.ShapeDtypeStruct(cards.shape, BF16),
            ),
            in_specs=[pl.BlockSpec(memory_space=pl.ANY)] * 5,
            out_specs=(pl.BlockSpec(memory_space=pl.ANY),) + (whole_vmem(),) * 4,
            scratch_shapes=[
                pltpu.VMEM((boards, hands), F32),
                pltpu.VMEM((boards, hands), jnp.int32),
                pltpu.VMEM((boards, hands), jnp.int32),
                pltpu.VMEM((boards, hands), jnp.int32),
                pltpu.VMEM((boards, padded), F32),
                pltpu.VMEM((LANES, padded), F32),
                pltpu.VMEM((boards, padded, padded), BF16),
                pltpu.SemaphoreType.DMA((5,)),
                pltpu.SemaphoreType.DMA((chunks,)),
            ],
            cost_estimate=pl.CostEstimate(
                flops=8 * boards * padded * padded,
                bytes_accessed=(boards + 1) * 2 * padded * padded,
                transcendentals=0,
            ),
            compiler_params=pltpu.CompilerParams(vmem_limit_bytes=40 * 2**20),
        )(
            reach_in.reshape(boards, hands),
            live,
            hand_rank.reshape(boards, hands),
            hand_bucket.reshape(boards, hands),
            cards,
        )
    with jax.named_scope("share_sums"):
        mine = pl.pallas_call(
            follow_kernel,
            out_shape=jax.ShapeDtypeStruct(mine.shape, mine.dtype),
            in_specs=[whole_vmem()] * 2,
            out_specs=whole_vmem(),
            input_output_aliases={0: 0},
            compiler_params=pltpu.CompilerParams(vmem_limit_bytes=SMALL),
        )(mine, token)
        swap = [(device, device ^ 1) for device in range(turns)]
        other = lax.ppermute(mine, "turn", swap)
    with jax.named_scope("boards"):
        river, partial = pl.pallas_call(
            functools.partial(board_kernel, blocks, in_code),
            out_shape=(
                jax.ShapeDtypeStruct((boards, entries, hands), F32),
                jax.ShapeDtypeStruct((rivers, entries, padded), I16),
            ),
            in_specs=[whole_vmem()] * 4 + [pl.BlockSpec(memory_space=pl.ANY)] * 2,
            out_specs=(pl.BlockSpec(memory_space=pl.ANY), whole_vmem()),
            scratch_shapes=[
                pltpu.VMEM((boards, padded, padded), BF16),
                pltpu.SMEM(slots.shape, jnp.int32),
                pltpu.VMEM((CORES * rivers * held_rows, LANES), F32),
                pltpu.VMEM((padded, LANES), F32),
                pltpu.VMEM((boards, LANES // blocks, padded), BF16),
                pltpu.VMEM((boards * LANES // blocks, padded), BF16),
                pltpu.VMEM((boards, entries, hands), F32),
                pltpu.SemaphoreType.DMA((boards,)),
                pltpu.SemaphoreType.DMA(()),
                pltpu.SemaphoreType.DMA((boards,)),
            ],
            compiler_params=pltpu.CompilerParams(vmem_limit_bytes=40 * 2**20),
        )(mine, other, hand_rows, cards, contest, slots)
    with jax.named_scope("means"):
        by_river = lax.all_to_all(partial, "river", split_axis=0, concat_axis=0, tiled=True)
        turn_value, partial = pl.pallas_call(
            functools.partial(river_mean_kernel, 1.0 / (rivers * rivers_here)),
            out_shape=(
                jax.ShapeDtypeStruct((entries, hands), F32),
                jax.ShapeDtypeStruct((turns, entries, padded), I16),
            ),
            in_specs=[whole_vmem()],
            out_specs=(whole_vmem(), whole_vmem()),
            compiler_params=pltpu.CompilerParams(vmem_limit_bytes=SMALL),
        )(by_river)
        by_turn = lax.all_to_all(partial, "turn", split_axis=0, concat_axis=0, tiled=True)
        turn_value, flop_value = pl.pallas_call(
            functools.partial(turn_mean_kernel, 1.0 / (turns * turns_here)),
            out_shape=(
                jax.ShapeDtypeStruct(turn_value.shape, F32),
                jax.ShapeDtypeStruct((entries, hands), F32),
            ),
            in_specs=[whole_vmem()] * 2,
            out_specs=(whole_vmem(), whole_vmem()),
            compiler_params=pltpu.CompilerParams(vmem_limit_bytes=SMALL),
        )(by_turn, turn_value)
    river_value = river.reshape(turns_here, rivers_here, entries, hands)
    return river_value, turn_value[None], flop_value


def solution(mesh):
    return jax.shard_map(
        local,
        mesh=mesh,
        in_specs=(
            P("turn", "river", None),
            P("turn", "river", None),
            P("turn", "river", None),
            P("turn", "river", None),
            P(("river", "bucket"), None),
            P("bucket", None),
            P("bucket"),
            P("bucket"),
        ),
        out_specs=(
            P("turn", "river", "bucket", None),
            P("turn", "bucket", None),
            P("bucket", None),
        ),
        check_vma=False,
    )
```

```python
import functools

import jax
import jax.numpy as jnp
import numpy as np
from jax import lax
from jax.experimental import pallas as pl
from jax.experimental.pallas import tpu as pltpu
from jax.sharding import PartitionSpec as P

OPTIONS = 2
REPLIES = 8
LANES = 128
CARDS = 52
TILE = 16
CORES = 2
CONTEST_PLACES = 8
SMALL = 8 * 2**20
F32 = jnp.float32
BF16 = jnp.bfloat16
I16 = jnp.int16
POT_MOST = 24.0
POT_LEAST = 2.0
CHANCE_LEAST = 0.049804688
CODE_MOST = 32000.0


def card_table(count, padded):
    table = np.zeros((LANES, padded), np.float32)
    for cards in np.triu_indices(CARDS, 1):
        table[cards[:count], np.arange(count)] = 1.0
    return jnp.asarray(table, BF16)


def code_scale(floor, most):
    return CODE_MOST / np.log2(1.0 + most / floor)


def sum_code(hands, depth):
    most = REPLIES * POT_MOST / hands
    floor = POT_LEAST / hands * CHANCE_LEAST**depth
    return floor, code_scale(floor, most)


def dither(rows, river):
    row = lax.broadcasted_iota(jnp.int32, (rows, LANES), 0)
    lane = lax.broadcasted_iota(jnp.int32, (rows, LANES), 1)
    place = (row * 3091 + lane * 2333 + river * 1697) & 4095
    return (place.astype(F32) + 0.5) * (1.0 / 4096)


def encode(x, offset, floor, scale):
    size = jnp.log(1.0 + jnp.abs(x) * (1.0 / floor)) * (scale / np.log(2.0))
    size = jnp.minimum(jnp.floor(size + offset), 32767.0)
    return jnp.where(x < 0, -size, size).astype(jnp.int32).astype(I16)


def decode(code, offset, floor, scale):
    code = code.astype(jnp.int32).astype(F32)
    size = (jnp.abs(code) + (0.5 - offset)) * (np.log(2.0) / scale)
    size = (jnp.exp(size) - 1.0) * floor
    return jnp.where(code == 0, 0.0, jnp.where(code < 0, -size, size))


def encode_rows(x, hands):
    most = jnp.maximum(jnp.max(jnp.abs(x), axis=1, keepdims=True), 1e-30)
    power = jnp.floor(jnp.log(most) * (1.0 / np.log(2.0)) + 1.0)
    code = jnp.floor(x * (jnp.exp(power * -np.log(2.0)) * CODE_MOST) + 0.5)
    lane = lax.broadcasted_iota(jnp.int32, x.shape, 1)
    return jnp.where(lane == hands, power, code).astype(jnp.int32).astype(I16)


def sum_decoded(codes_ref, hands):
    total = None
    for index in range(codes_ref.shape[0]):
        code = codes_ref[index].astype(jnp.int32).astype(F32)
        step = jnp.exp(code[:, hands : hands + 1] * np.log(2.0)) * (1.0 / CODE_MOST)
        part = code * step
        total = part if total is None else total + part
    return total


def split_two(x):
    high = x.astype(BF16)
    return high, (x - high.astype(F32)).astype(BF16)


def split_three(x):
    high = x.astype(BF16)
    rest = x - high.astype(F32)
    middle = rest.astype(BF16)
    return high, middle, (rest - middle.astype(F32)).astype(BF16)


def dot_rows(a, b):
    return lax.dot_general(a, b, (((1,), (1,)), ((), ())), preferred_element_type=F32)


def line_sum_kernel(hand_count, code, rows_ref, info_ref, sums_ref):
    blocks, rows, width = rows_ref.shape
    depth, lines = info_ref.shape
    depth -= 2
    entries = lines // (OPTIONS * REPLIES)
    table = [rows_ref[block].astype(F32) for block in range(blocks)]
    table = jnp.concatenate(table, axis=0).astype(BF16)
    column = lax.broadcasted_iota(jnp.int32, (width, lines), 0).astype(F32)
    picks = [
        (column == info_ref[step : step + 1, :]).astype(F32).astype(BF16) for step in range(depth)
    ]
    picks = jnp.concatenate(picks, axis=1)
    present = jnp.dot(jnp.ones((8, width), BF16), picks, preferred_element_type=F32)
    looked = jnp.dot(table, picks, preferred_element_type=F32) + (1.0 - present[0:1])
    product = looked[:, 0:lines]
    for step in range(1, depth):
        product = product * looked[:, step * lines : (step + 1) * lines]
    kind = info_ref[depth : depth + 1, :]
    scale = info_ref[depth + 1 : depth + 2, :] / hand_count
    sign = jnp.where(kind == 1.0, 1.0, jnp.where(kind == 2.0, -1.0, 0.0))
    weights = (jnp.where(kind == 0.0, scale, 0.0), sign * scale)
    line = lax.broadcasted_iota(jnp.int32, (lines, LANES), 0)
    lane = lax.broadcasted_iota(jnp.int32, (lines, LANES), 1)
    slot = ((line // REPLIES) % OPTIONS) * entries + line // (REPLIES * OPTIONS)
    group = OPTIONS * entries
    terms, targets = [], []
    for kind_index, weight in enumerate(weights):
        terms.extend(split_three(product * weight))
        targets.extend([(lane == slot + kind_index * group).astype(F32).astype(BF16)] * 3)
    summed = jnp.dot(
        jnp.concatenate(terms, axis=1),
        jnp.concatenate(targets, axis=0),
        preferred_element_type=F32,
    )
    total = summed[0:rows]
    for block in range(1, blocks):
        part = summed[block * rows : (block + 1) * rows]
        total += pltpu.roll(part, block * 2 * group, 1)
    codes = encode(total, dither(rows, lax.axis_index("river")), *code)
    for copy in range(sums_ref.shape[0]):
        sums_ref[copy] = codes


def prepare_kernel(
    shard_rows, held_rows, blocks, rivers, reach_hbm, live_hbm, rank_hbm, bucket_hbm,
    cards_hbm, contest_hbm, rows_ref, slots_ref, token_ref, cards_ref, reach_ref, live_ref, rank_ref,
    bucket_ref, index_ref, turned_ref, contest_ref, in_sems, sems,
):
    arrays = (reach_hbm, live_hbm, rank_hbm, bucket_hbm, cards_hbm)
    places = (reach_ref, live_ref, rank_ref, bucket_ref, cards_ref)
    copies = []
    for index, (array, place) in enumerate(zip(arrays, places)):
        copies.append(pltpu.make_async_copy(array, place, in_sems.at[index]))
        copies[-1].start()
    boards, hands = reach_ref.shape
    padded = cards_ref.shape[1]
    chunks = padded // LANES
    token_ref[...] = jnp.zeros(token_ref.shape, I16)
    for copy in copies:
        copy.wait()
    bucket = bucket_ref[...].astype(F32)
    owner = jnp.floor((bucket + 0.5) * (1.0 / shard_rows))
    row = bucket - owner * shard_rows
    place = jnp.floor((owner + 0.5) * (1.0 / blocks))
    half = jnp.where(row >= held_rows, 1.0, 0.0)
    row = row - half * (shard_rows - held_rows)
    core = lax.rem(lax.axis_index("turn"), CORES).astype(F32)
    elsewhere = jnp.where(half == core, 0.0, 1.0)
    index_ref[...] = jnp.zeros(index_ref.shape, F32)
    index_ref[:, 0:hands] = (elsewhere * rivers + place) * held_rows + row
    slots_ref[...] = jnp.zeros(slots_ref.shape, jnp.int32)
    for board in range(boards):
        for chunk in range(chunks):
            slot = index_ref[board : board + 1, chunk * LANES : (chunk + 1) * LANES]
            at = board * chunks + chunk
            slots_ref[at : at + 1, :] = slot.astype(jnp.int32)
    rows_ref[...] = jnp.zeros(rows_ref.shape, F32)
    rows_ref[0:boards, 0:hands] = owner - place * blocks
    live = live_ref[...].astype(F32)
    rows_ref[boards : 2 * boards, 0:hands] = reach_ref[...] * live
    rows_ref[2 * boards : 3 * boards, 0:hands] = live

    turned_ref[...] = jnp.zeros(turned_ref.shape, F32)
    turned_ref[0:boards, 0:hands] = rank_ref[...].astype(F32)
    rank_rows = turned_ref[0:8, :]
    copies = []
    for chunk in range(chunks):
        lines = pl.ds(chunk * LANES, LANES)
        ranks = turned_ref[:, lines].T
        cards = cards_ref[:, lines].astype(F32).T.astype(BF16)
        shared = jnp.dot(cards, cards_ref[...], preferred_element_type=F32)
        for board in range(boards):
            order = rank_rows[board : board + 1, :] - ranks[:, board : board + 1]
            contest = jnp.where(shared == 0.0, jnp.clip(order, -1.0, 1.0), 0.0)
            contest_ref[board, lines, :] = contest.astype(BF16)
        copy = pltpu.make_async_copy(
            contest_ref.at[:, lines, :], contest_hbm.at[0:boards, lines, :], sems.at[chunk]
        )
        copy.start()
        copies.append(copy)
    around = cards_ref[TILE * (CARDS // TILE) : TILE * (CARDS // TILE + 1), :].astype(F32)
    row = lax.broadcasted_iota(jnp.int32, around.shape, 0)
    around = jnp.where(row == CARDS % TILE, 1.0, around).astype(BF16)
    cards_ref[TILE * (CARDS // TILE) : TILE * (CARDS // TILE + 1), :] = around
    for copy in copies:
        copy.wait()


def board_kernel(
    blocks, in_code, mine_ref, other_ref, rows_ref, cards_ref, contest_hbm, slots_hbm, river_hbm,
    part_ref, contest_ref, slots_ref, plain_ref, found_ref, show_ref, fold_ref, river_ref,
    contest_sems, slots_sem, river_sems,
):
    boards, _, hands = river_ref.shape
    padded = cards_ref.shape[1]
    chunks = padded // LANES
    rivers, held_rows, _ = mine_ref.shape
    columns = LANES // blocks
    half = columns // 2
    entries = half // OPTIONS
    slots_copy = pltpu.make_async_copy(slots_hbm, slots_ref, slots_sem)
    slots_copy.start()
    contest_copies = []
    for board in range(boards):
        contest_copies.append(
            pltpu.make_async_copy(
                contest_hbm.at[board], contest_ref.at[board], contest_sems.at[board]
            )
        )
        contest_copies[board].start()

    for river in range(rivers):
        offset = dither(held_rows, river)
        for part, ref in enumerate((mine_ref, other_ref)):
            at = (part * rivers + river) * held_rows
            plain_ref[at : at + held_rows, :] = decode(ref[river], offset, *in_code)
    slots_copy.wait()

    for board in range(boards):

        def gather(chunk, carry, board=board):
            base = pl.multiple_of(chunk * LANES, LANES)
            for hand in range(LANES):
                slot = slots_ref[board * chunks + chunk, hand]
                found_ref[pl.ds(base + hand, 1), :] = plain_ref[pl.ds(slot, 1), :]
            return carry

        lax.fori_loop(0, chunks, gather, 0)

        for chunk in range(chunks):
            lanes = pl.ds(chunk * LANES, LANES)
            found = found_ref[lanes, :].T
            group = rows_ref[board : board + 1, lanes]
            reach = rows_ref[boards + board : boards + board + 1, lanes]
            chosen = jnp.zeros((columns, LANES), F32)
            for which in range(blocks):
                chosen += jnp.where(
                    group == which, found[which * columns : (which + 1) * columns], 0.0
                )
            high, low = split_two(chosen * reach)
            show_ref[board, 0:half, lanes] = high[0:half]
            show_ref[board, half:columns, lanes] = low[0:half]
            base = board * half
            fold_ref[base : base + half, lanes] = high[half:columns]
            base = (boards + board) * half
            fold_ref[base : base + half, lanes] = low[half:columns]

    cards = cards_ref[...]
    folds = fold_ref[...]
    held_by = dot_rows(folds, cards)
    held_by = held_by[0 : boards * half] + held_by[boards * half : 2 * boards * half]
    lane = lax.broadcasted_iota(jnp.int32, held_by.shape, 1)
    held_by = jnp.where(lane == CARDS, held_by, -held_by)
    spread = jnp.dot(
        jnp.concatenate(split_three(held_by), axis=0), cards, preferred_element_type=F32
    )
    folded = folds[0 : boards * half].astype(F32) + folds[boards * half :].astype(F32)
    for piece in range(3):
        folded += spread[piece * boards * half : (piece + 1) * boards * half]
    total = None
    river_copies = []
    for board in range(boards):
        contest_copies[board].wait()
        shown = jnp.dot(show_ref[board], contest_ref[board], preferred_element_type=F32)
        value = shown[0:half] + shown[half:columns] + folded[board * half : (board + 1) * half]
        best = jnp.maximum(value[0:entries], value[entries:half])
        best = best * rows_ref[2 * boards + board : 2 * boards + board + 1, :]
        river_ref[board] = best[:, 0:hands]
        river_copies.append(
            pltpu.make_async_copy(river_ref.at[board], river_hbm.at[board], river_sems.at[board])
        )
        river_copies[board].start()
        total = best if total is None else total + best
    codes = encode_rows(total, hands)
    for copy in range(part_ref.shape[0]):
        part_ref[copy] = codes
    for copy in river_copies:
        copy.wait()


def river_mean_kernel(share, codes_ref, mean_ref, part_ref):
    hands = mean_ref.shape[1]
    mean = sum_decoded(codes_ref, hands) * share
    mean_ref[...] = mean[:, 0:hands]
    lane = lax.broadcasted_iota(jnp.int32, mean.shape, 1)
    codes = encode_rows(jnp.where(lane < hands, mean, 0.0), hands)
    for copy in range(part_ref.shape[0]):
        part_ref[copy] = codes


def turn_mean_kernel(share, codes_ref, turn_ref, turn_out_ref, mean_ref):
    hands = mean_ref.shape[1]
    turn_out_ref[...] = turn_ref[...]
    mean_ref[...] = sum_decoded(codes_ref, hands)[:, 0:hands] * share


def follow_kernel(value_ref, token_ref, out_ref):
    del value_ref, token_ref, out_ref


def whole_vmem():
    return pl.BlockSpec(memory_space=pltpu.VMEM)


def local(reach_in, hand_live, hand_rank, hand_bucket, strategy, line_acts, line_kind, line_pot):
    turns_here, rivers_here, hands = reach_in.shape
    boards = turns_here * rivers_here
    shard_rows, width = strategy.shape
    lines = line_acts.shape[0]
    entries = lines // (OPTIONS * REPLIES)
    blocks = lax.axis_size("bucket")
    rivers = lax.axis_size("river")
    turns = lax.axis_size("turn")
    padded = -(-hands // LANES) * LANES
    held_rows = -(-shard_rows // (CORES * 8)) * 8
    core = lax.axis_index("turn") % CORES

    with jax.named_scope("share_rows"):
        first = core * (shard_rows - held_rows)
        part = lax.dynamic_slice_in_dim(strategy, first, held_rows, axis=0)
        rows = lax.all_to_all(
            jnp.broadcast_to(part[None], (blocks, held_rows, width)),
            "bucket",
            split_axis=0,
            concat_axis=0,
            tiled=True,
        )
    in_code = sum_code(hands, line_acts.shape[1])
    info = [line_acts.T.astype(F32), line_kind.astype(F32)[None], line_pot[None]]
    info = jnp.concatenate(info, axis=0)
    with jax.named_scope("line_sums"):
        sums = pl.pallas_call(
            functools.partial(line_sum_kernel, hands, in_code),
            out_shape=jax.ShapeDtypeStruct((rivers, held_rows, LANES), I16),
            in_specs=[whole_vmem()] * 2,
            out_specs=whole_vmem(),
            compiler_params=pltpu.CompilerParams(vmem_limit_bytes=16 * 2**20),
        )(rows, info)
    cards = card_table(hands, padded)
    live = hand_live.reshape(boards, hands)
    with jax.named_scope("share_sums"):
        mine = lax.all_to_all(sums, "river", split_axis=0, concat_axis=0, tiled=True)
    with jax.named_scope("prepare"):
        chunks = padded // LANES
        slot_shape = (-(-boards * chunks // 8) * 8, LANES)
        contest, hand_rows, slots, token, cards = pl.pallas_call(
            functools.partial(prepare_kernel, shard_rows, held_rows, blocks, rivers),
            out_shape=(
                jax.ShapeDtypeStruct((CONTEST_PLACES, padded, padded), BF16),
                jax.ShapeDtypeStruct((8, padded), F32),
                jax.ShapeDtypeStruct(slot_shape, jnp.int32),
                jax.ShapeDtypeStruct((16, LANES), I16),
                jax.ShapeDtypeStruct(cards.shape, BF16),
            ),
            in_specs=[pl.BlockSpec(memory_space=pl.ANY)] * 5,
            out_specs=(pl.BlockSpec(memory_space=pl.ANY),) + (whole_vmem(),) * 4,
            scratch_shapes=[
                pltpu.VMEM((boards, hands), F32),
                pltpu.VMEM((boards, hands), jnp.int32),
                pltpu.VMEM((boards, hands), jnp.int32),
                pltpu.VMEM((boards, hands), jnp.int32),
                pltpu.VMEM((boards, padded), F32),
                pltpu.VMEM((LANES, padded), F32),
                pltpu.VMEM((boards, padded, padded), BF16),
                pltpu.SemaphoreType.DMA((5,)),
                pltpu.SemaphoreType.DMA((chunks,)),
            ],
            cost_estimate=pl.CostEstimate(
                flops=8 * boards * padded * padded,
                bytes_accessed=(boards + 1) * 2 * padded * padded,
                transcendentals=0,
            ),
            compiler_params=pltpu.CompilerParams(vmem_limit_bytes=40 * 2**20),
        )(
            reach_in.reshape(boards, hands),
            live,
            hand_rank.reshape(boards, hands),
            hand_bucket.reshape(boards, hands),
            cards,
        )
    with jax.named_scope("share_sums"):
        mine = pl.pallas_call(
            follow_kernel,
            out_shape=jax.ShapeDtypeStruct(mine.shape, mine.dtype),
            in_specs=[whole_vmem()] * 2,
            out_specs=whole_vmem(),
            input_output_aliases={0: 0},
            compiler_params=pltpu.CompilerParams(vmem_limit_bytes=SMALL),
        )(mine, token)
        swap = [(device, device ^ 1) for device in range(turns)]
        other = lax.ppermute(mine, "turn", swap)
    with jax.named_scope("boards"):
        river, partial = pl.pallas_call(
            functools.partial(board_kernel, blocks, in_code),
            out_shape=(
                jax.ShapeDtypeStruct((boards, entries, hands), F32),
                jax.ShapeDtypeStruct((rivers, entries, padded), I16),
            ),
            in_specs=[whole_vmem()] * 4 + [pl.BlockSpec(memory_space=pl.ANY)] * 2,
            out_specs=(pl.BlockSpec(memory_space=pl.ANY), whole_vmem()),
            scratch_shapes=[
                pltpu.VMEM((boards, padded, padded), BF16),
                pltpu.SMEM(slots.shape, jnp.int32),
                pltpu.VMEM((CORES * rivers * held_rows, LANES), F32),
                pltpu.VMEM((padded, LANES), F32),
                pltpu.VMEM((boards, LANES // blocks, padded), BF16),
                pltpu.VMEM((boards * LANES // blocks, padded), BF16),
                pltpu.VMEM((boards, entries, hands), F32),
                pltpu.SemaphoreType.DMA((boards,)),
                pltpu.SemaphoreType.DMA(()),
                pltpu.SemaphoreType.DMA((boards,)),
            ],
            compiler_params=pltpu.CompilerParams(vmem_limit_bytes=40 * 2**20),
        )(mine, other, hand_rows, cards, contest, slots)
    with jax.named_scope("means"):
        by_river = lax.all_to_all(partial, "river", split_axis=0, concat_axis=0, tiled=True)
        turn_value, partial = pl.pallas_call(
            functools.partial(river_mean_kernel, 1.0 / (rivers * rivers_here)),
            out_shape=(
                jax.ShapeDtypeStruct((entries, hands), F32),
                jax.ShapeDtypeStruct((turns, entries, padded), I16),
            ),
            in_specs=[whole_vmem()],
            out_specs=(whole_vmem(), whole_vmem()),
            compiler_params=pltpu.CompilerParams(vmem_limit_bytes=SMALL),
        )(by_river)
        by_turn = lax.all_to_all(partial, "turn", split_axis=0, concat_axis=0, tiled=True)
        turn_value, flop_value = pl.pallas_call(
            functools.partial(turn_mean_kernel, 1.0 / (turns * turns_here)),
            out_shape=(
                jax.ShapeDtypeStruct(turn_value.shape, F32),
                jax.ShapeDtypeStruct((entries, hands), F32),
            ),
            in_specs=[whole_vmem()] * 2,
            out_specs=(whole_vmem(), whole_vmem()),
            compiler_params=pltpu.CompilerParams(vmem_limit_bytes=SMALL),
        )(by_turn, turn_value)
    river_value = river.reshape(turns_here, rivers_here, entries, hands)
    return river_value, turn_value[None], flop_value


def solution(mesh):
    return jax.shard_map(
        local,
        mesh=mesh,
        in_specs=(
            P("turn", "river", None),
            P("turn", "river", None),
            P("turn", "river", None),
            P("turn", "river", None),
            P(("river", "bucket"), None),
            P("bucket", None),
            P("bucket"),
            P("bucket"),
        ),
        out_specs=(
            P("turn", "river", "bucket", None),
            P("turn", "bucket", None),
            P("bucket", None),
        ),
        check_vma=False,
    )
```

```python
import functools

import jax
import jax.numpy as jnp
import numpy as np
from jax import lax
from jax.experimental import pallas as pl
from jax.experimental.pallas import tpu as pltpu
from jax.sharding import PartitionSpec as P

OPTIONS = 2
REPLIES = 8
LANES = 128
CARDS = 52
TILE = 16
CORES = 2
CONTEST_PLACES = 8
SMALL = 8 * 2**20
F32 = jnp.float32
BF16 = jnp.bfloat16
I16 = jnp.int16
POT_MOST = 24.0
POT_LEAST = 2.0
CHANCE_LEAST = 0.049804688
CODE_MOST = 32000.0


def card_table(count, padded):
    table = np.zeros((LANES, padded), np.float32)
    for cards in np.triu_indices(CARDS, 1):
        table[cards[:count], np.arange(count)] = 1.0
    return jnp.asarray(table, BF16)


def code_scale(floor, most):
    return CODE_MOST / np.log2(1.0 + most / floor)


def sum_code(hands, depth):
    most = REPLIES * POT_MOST / hands
    floor = POT_LEAST / hands * CHANCE_LEAST**depth
    return floor, code_scale(floor, most)


def dither(rows, river):
    row = lax.broadcasted_iota(jnp.int32, (rows, LANES), 0)
    lane = lax.broadcasted_iota(jnp.int32, (rows, LANES), 1)
    place = (row * 3091 + lane * 2333 + river * 1697) & 4095
    return (place.astype(F32) + 0.5) * (1.0 / 4096)


def encode(x, offset, floor, scale):
    size = jnp.log(1.0 + jnp.abs(x) * (1.0 / floor)) * (scale / np.log(2.0))
    size = jnp.minimum(jnp.floor(size + offset), 32767.0)
    return jnp.where(x < 0, -size, size).astype(jnp.int32).astype(I16)


def decode(code, offset, floor, scale):
    code = code.astype(jnp.int32).astype(F32)
    size = (jnp.abs(code) + (0.5 - offset)) * (np.log(2.0) / scale)
    size = (jnp.exp(size) - 1.0) * floor
    return jnp.where(code == 0, 0.0, jnp.where(code < 0, -size, size))


def encode_rows(x, hands):
    most = jnp.maximum(jnp.max(jnp.abs(x), axis=1, keepdims=True), 1e-30)
    power = jnp.floor(jnp.log(most) * (1.0 / np.log(2.0)) + 1.0)
    code = jnp.floor(x * (jnp.exp(power * -np.log(2.0)) * CODE_MOST) + 0.5)
    lane = lax.broadcasted_iota(jnp.int32, x.shape, 1)
    return jnp.where(lane == hands, power, code).astype(jnp.int32).astype(I16)


def sum_decoded(codes_ref, hands):
    total = None
    for index in range(codes_ref.shape[0]):
        code = codes_ref[index].astype(jnp.int32).astype(F32)
        step = jnp.exp(code[:, hands : hands + 1] * np.log(2.0)) * (1.0 / CODE_MOST)
        part = code * step
        total = part if total is None else total + part
    return total


def split_two(x):
    high = x.astype(BF16)
    return high, (x - high.astype(F32)).astype(BF16)


def split_three(x):
    high = x.astype(BF16)
    rest = x - high.astype(F32)
    middle = rest.astype(BF16)
    return high, middle, (rest - middle.astype(F32)).astype(BF16)


def dot_rows(a, b):
    return lax.dot_general(a, b, (((1,), (1,)), ((), ())), preferred_element_type=F32)


def line_sum_kernel(hand_count, code, rows_ref, info_ref, sums_ref):
    blocks, rows, width = rows_ref.shape
    depth, lines = info_ref.shape
    depth -= 2
    entries = lines // (OPTIONS * REPLIES)
    table = [rows_ref[block].astype(F32) for block in range(blocks)]
    table = jnp.concatenate(table, axis=0).astype(BF16)
    column = lax.broadcasted_iota(jnp.int32, (width, lines), 0).astype(F32)
    picks = [
        (column == info_ref[step : step + 1, :]).astype(F32).astype(BF16) for step in range(depth)
    ]
    picks = jnp.concatenate(picks, axis=1)
    present = jnp.dot(jnp.ones((8, width), BF16), picks, preferred_element_type=F32)
    looked = jnp.dot(table, picks, preferred_element_type=F32) + (1.0 - present[0:1])
    product = looked[:, 0:lines]
    for step in range(1, depth):
        product = product * looked[:, step * lines : (step + 1) * lines]
    kind = info_ref[depth : depth + 1, :]
    scale = info_ref[depth + 1 : depth + 2, :] / hand_count
    sign = jnp.where(kind == 1.0, 1.0, jnp.where(kind == 2.0, -1.0, 0.0))
    weights = (jnp.where(kind == 0.0, scale, 0.0), sign * scale)
    line = lax.broadcasted_iota(jnp.int32, (lines, LANES), 0)
    lane = lax.broadcasted_iota(jnp.int32, (lines, LANES), 1)
    slot = ((line // REPLIES) % OPTIONS) * entries + line // (REPLIES * OPTIONS)
    group = OPTIONS * entries
    terms, targets = [], []
    for kind_index, weight in enumerate(weights):
        terms.extend(split_three(product * weight))
        targets.extend([(lane == slot + kind_index * group).astype(F32).astype(BF16)] * 3)
    summed = jnp.dot(
        jnp.concatenate(terms, axis=1),
        jnp.concatenate(targets, axis=0),
        preferred_element_type=F32,
    )
    total = summed[0:rows]
    for block in range(1, blocks):
        part = summed[block * rows : (block + 1) * rows]
        total += pltpu.roll(part, block * 2 * group, 1)
    codes = encode(total, dither(rows, lax.axis_index("river")), *code)
    for copy in range(sums_ref.shape[0]):
        sums_ref[copy] = codes


def prepare_kernel(
    shard_rows, held_rows, blocks, rivers, reach_hbm, live_hbm, rank_hbm, bucket_hbm,
    cards_hbm, contest_hbm, rows_ref, slots_ref, token_ref, cards_ref, reach_ref, live_ref, rank_ref,
    bucket_ref, index_ref, turned_ref, contest_ref, in_sems, sems,
):
    arrays = (reach_hbm, live_hbm, rank_hbm, bucket_hbm, cards_hbm)
    places = (reach_ref, live_ref, rank_ref, bucket_ref, cards_ref)
    copies = []
    for index, (array, place) in enumerate(zip(arrays, places)):
        copies.append(pltpu.make_async_copy(array, place, in_sems.at[index]))
        copies[-1].start()
    boards, hands = reach_ref.shape
    padded = cards_ref.shape[1]
    chunks = padded // LANES
    token_ref[...] = jnp.zeros(token_ref.shape, I16)
    for copy in copies:
        copy.wait()
    bucket = bucket_ref[...].astype(F32)
    owner = jnp.floor((bucket + 0.5) * (1.0 / shard_rows))
    row = bucket - owner * shard_rows
    place = jnp.floor((owner + 0.5) * (1.0 / blocks))
    half = jnp.where(row >= held_rows, 1.0, 0.0)
    row = row - half * (shard_rows - held_rows)
    core = lax.rem(lax.axis_index("turn"), CORES).astype(F32)
    elsewhere = jnp.where(half == core, 0.0, 1.0)
    index_ref[...] = jnp.zeros(index_ref.shape, F32)
    index_ref[:, 0:hands] = (elsewhere * rivers + place) * held_rows + row
    slots_ref[...] = jnp.zeros(slots_ref.shape, jnp.int32)
    for board in range(boards):
        for chunk in range(chunks):
            slot = index_ref[board : board + 1, chunk * LANES : (chunk + 1) * LANES]
            at = board * chunks + chunk
            slots_ref[at : at + 1, :] = slot.astype(jnp.int32)
    rows_ref[...] = jnp.zeros(rows_ref.shape, F32)
    rows_ref[0:boards, 0:hands] = owner - place * blocks
    live = live_ref[...].astype(F32)
    rows_ref[boards : 2 * boards, 0:hands] = reach_ref[...] * live
    rows_ref[2 * boards : 3 * boards, 0:hands] = live

    turned_ref[...] = jnp.zeros(turned_ref.shape, F32)
    turned_ref[0:boards, 0:hands] = rank_ref[...].astype(F32)
    rank_rows = turned_ref[0:8, :]
    copies = []
    for chunk in range(chunks):
        lines = pl.ds(chunk * LANES, LANES)
        ranks = turned_ref[:, lines].T
        cards = cards_ref[:, lines].astype(F32).T.astype(BF16)
        shared = jnp.dot(cards, cards_ref[...], preferred_element_type=F32)
        for board in range(boards):
            order = rank_rows[board : board + 1, :] - ranks[:, board : board + 1]
            contest = jnp.where(shared == 0.0, jnp.clip(order, -1.0, 1.0), 0.0)
            contest_ref[board, lines, :] = contest.astype(BF16)
        copy = pltpu.make_async_copy(
            contest_ref.at[:, lines, :], contest_hbm.at[0:boards, lines, :], sems.at[chunk]
        )
        copy.start()
        copies.append(copy)
    around = cards_ref[TILE * (CARDS // TILE) : TILE * (CARDS // TILE + 1), :].astype(F32)
    row = lax.broadcasted_iota(jnp.int32, around.shape, 0)
    around = jnp.where(row == CARDS % TILE, 1.0, around).astype(BF16)
    cards_ref[TILE * (CARDS // TILE) : TILE * (CARDS // TILE + 1), :] = around
    for copy in copies:
        copy.wait()


def board_kernel(
    blocks, in_code, mine_ref, other_ref, rows_ref, cards_ref, contest_hbm, slots_hbm, river_hbm,
    part_ref, contest_ref, slots_ref, plain_ref, found_ref, show_ref, fold_ref, river_ref,
    contest_sems, slots_sem, river_sems,
):
    boards, _, hands = river_ref.shape
    padded = cards_ref.shape[1]
    chunks = padded // LANES
    rivers, held_rows, _ = mine_ref.shape
    columns = LANES // blocks
    half = columns // 2
    entries = half // OPTIONS
    slots_copy = pltpu.make_async_copy(slots_hbm, slots_ref, slots_sem)
    slots_copy.start()
    contest_copies = []
    for board in range(boards):
        contest_copies.append(
            pltpu.make_async_copy(
                contest_hbm.at[board], contest_ref.at[board], contest_sems.at[board]
            )
        )
        contest_copies[board].start()

    for river in range(rivers):
        offset = dither(held_rows, river)
        for part, ref in enumerate((mine_ref, other_ref)):
            at = (part * rivers + river) * held_rows
            plain_ref[at : at + held_rows, :] = decode(ref[river], offset, *in_code)
    slots_copy.wait()

    def place(board, chunk):
        lanes = pl.ds(pl.multiple_of(chunk * LANES, LANES), LANES)
        found = found_ref[lanes, :].T
        group = rows_ref[board : board + 1, lanes]
        reach = rows_ref[boards + board : boards + board + 1, lanes]
        chosen = jnp.zeros((columns, LANES), F32)
        for which in range(blocks):
            chosen += jnp.where(
                group == which, found[which * columns : (which + 1) * columns], 0.0
            )
        high, low = split_two(chosen * reach)
        show_ref[board, 0:half, lanes] = high[0:half]
        show_ref[board, half:columns, lanes] = low[0:half]
        base = board * half
        fold_ref[base : base + half, lanes] = high[half:columns]
        base = (boards + board) * half
        fold_ref[base : base + half, lanes] = low[half:columns]

    def find(board, chunk):
        base = pl.multiple_of(chunk * LANES, LANES)
        for hand in range(LANES):
            slot = slots_ref[board * chunks + chunk, hand]
            found_ref[pl.ds(base + hand, 1), :] = plain_ref[pl.ds(slot, 1), :]

    for board in range(boards):
        find(board, 0)

        def gather(chunk, carry, board=board):
            place(board, chunk - 1)
            find(board, chunk)
            return carry

        lax.fori_loop(1, chunks, gather, 0)
        place(board, chunks - 1)

    cards = cards_ref[...]
    folds = fold_ref[...]
    held_by = dot_rows(folds, cards)
    held_by = held_by[0 : boards * half] + held_by[boards * half : 2 * boards * half]
    lane = lax.broadcasted_iota(jnp.int32, held_by.shape, 1)
    held_by = jnp.where(lane == CARDS, held_by, -held_by)
    spread = jnp.dot(
        jnp.concatenate(split_three(held_by), axis=0), cards, preferred_element_type=F32
    )
    folded = folds[0 : boards * half].astype(F32) + folds[boards * half :].astype(F32)
    for piece in range(3):
        folded += spread[piece * boards * half : (piece + 1) * boards * half]
    total = None
    river_copies = []
    for board in range(boards):
        contest_copies[board].wait()
        shown = jnp.dot(show_ref[board], contest_ref[board], preferred_element_type=F32)
        value = shown[0:half] + shown[half:columns] + folded[board * half : (board + 1) * half]
        best = jnp.maximum(value[0:entries], value[entries:half])
        best = best * rows_ref[2 * boards + board : 2 * boards + board + 1, :]
        river_ref[board] = best[:, 0:hands]
        river_copies.append(
            pltpu.make_async_copy(river_ref.at[board], river_hbm.at[board], river_sems.at[board])
        )
        river_copies[board].start()
        total = best if total is None else total + best
    codes = encode_rows(total, hands)
    for copy in range(part_ref.shape[0]):
        part_ref[copy] = codes
    for copy in river_copies:
        copy.wait()


def river_mean_kernel(share, codes_ref, mean_ref, part_ref):
    hands = mean_ref.shape[1]
    mean = sum_decoded(codes_ref, hands) * share
    mean_ref[...] = mean[:, 0:hands]
    lane = lax.broadcasted_iota(jnp.int32, mean.shape, 1)
    codes = encode_rows(jnp.where(lane < hands, mean, 0.0), hands)
    for copy in range(part_ref.shape[0]):
        part_ref[copy] = codes


def turn_mean_kernel(share, codes_ref, turn_ref, turn_out_ref, mean_ref):
    hands = mean_ref.shape[1]
    turn_out_ref[...] = turn_ref[...]
    mean_ref[...] = sum_decoded(codes_ref, hands)[:, 0:hands] * share


def follow_kernel(value_ref, token_ref, out_ref):
    del value_ref, token_ref, out_ref


def whole_vmem():
    return pl.BlockSpec(memory_space=pltpu.VMEM)


def local(reach_in, hand_live, hand_rank, hand_bucket, strategy, line_acts, line_kind, line_pot):
    turns_here, rivers_here, hands = reach_in.shape
    boards = turns_here * rivers_here
    shard_rows, width = strategy.shape
    lines = line_acts.shape[0]
    entries = lines // (OPTIONS * REPLIES)
    blocks = lax.axis_size("bucket")
    rivers = lax.axis_size("river")
    turns = lax.axis_size("turn")
    padded = -(-hands // LANES) * LANES
    held_rows = -(-shard_rows // (CORES * 8)) * 8
    core = lax.axis_index("turn") % CORES

    with jax.named_scope("share_rows"):
        first = core * (shard_rows - held_rows)
        part = lax.dynamic_slice_in_dim(strategy, first, held_rows, axis=0)
        rows = lax.all_to_all(
            jnp.broadcast_to(part[None], (blocks, held_rows, width)),
            "bucket",
            split_axis=0,
            concat_axis=0,
            tiled=True,
        )
    in_code = sum_code(hands, line_acts.shape[1])
    info = [line_acts.T.astype(F32), line_kind.astype(F32)[None], line_pot[None]]
    info = jnp.concatenate(info, axis=0)
    with jax.named_scope("line_sums"):
        sums = pl.pallas_call(
            functools.partial(line_sum_kernel, hands, in_code),
            out_shape=jax.ShapeDtypeStruct((rivers, held_rows, LANES), I16),
            in_specs=[whole_vmem()] * 2,
            out_specs=whole_vmem(),
            compiler_params=pltpu.CompilerParams(vmem_limit_bytes=16 * 2**20),
        )(rows, info)
    cards = card_table(hands, padded)
    live = hand_live.reshape(boards, hands)
    with jax.named_scope("share_sums"):
        mine = lax.all_to_all(sums, "river", split_axis=0, concat_axis=0, tiled=True)
    with jax.named_scope("prepare"):
        chunks = padded // LANES
        slot_shape = (-(-boards * chunks // 8) * 8, LANES)
        contest, hand_rows, slots, token, cards = pl.pallas_call(
            functools.partial(prepare_kernel, shard_rows, held_rows, blocks, rivers),
            out_shape=(
                jax.ShapeDtypeStruct((CONTEST_PLACES, padded, padded), BF16),
                jax.ShapeDtypeStruct((8, padded), F32),
                jax.ShapeDtypeStruct(slot_shape, jnp.int32),
                jax.ShapeDtypeStruct((16, LANES), I16),
                jax.ShapeDtypeStruct(cards.shape, BF16),
            ),
            in_specs=[pl.BlockSpec(memory_space=pl.ANY)] * 5,
            out_specs=(pl.BlockSpec(memory_space=pl.ANY),) + (whole_vmem(),) * 4,
            scratch_shapes=[
                pltpu.VMEM((boards, hands), F32),
                pltpu.VMEM((boards, hands), jnp.int32),
                pltpu.VMEM((boards, hands), jnp.int32),
                pltpu.VMEM((boards, hands), jnp.int32),
                pltpu.VMEM((boards, padded), F32),
                pltpu.VMEM((LANES, padded), F32),
                pltpu.VMEM((boards, padded, padded), BF16),
                pltpu.SemaphoreType.DMA((5,)),
                pltpu.SemaphoreType.DMA((chunks,)),
            ],
            cost_estimate=pl.CostEstimate(
                flops=8 * boards * padded * padded,
                bytes_accessed=(boards + 1) * 2 * padded * padded,
                transcendentals=0,
            ),
            compiler_params=pltpu.CompilerParams(vmem_limit_bytes=40 * 2**20),
        )(
            reach_in.reshape(boards, hands),
            live,
            hand_rank.reshape(boards, hands),
            hand_bucket.reshape(boards, hands),
            cards,
        )
    with jax.named_scope("share_sums"):
        mine = pl.pallas_call(
            follow_kernel,
            out_shape=jax.ShapeDtypeStruct(mine.shape, mine.dtype),
            in_specs=[whole_vmem()] * 2,
            out_specs=whole_vmem(),
            input_output_aliases={0: 0},
            compiler_params=pltpu.CompilerParams(vmem_limit_bytes=SMALL),
        )(mine, token)
        swap = [(device, device ^ 1) for device in range(turns)]
        other = lax.ppermute(mine, "turn", swap)
    with jax.named_scope("boards"):
        river, partial = pl.pallas_call(
            functools.partial(board_kernel, blocks, in_code),
            out_shape=(
                jax.ShapeDtypeStruct((boards, entries, hands), F32),
                jax.ShapeDtypeStruct((rivers, entries, padded), I16),
            ),
            in_specs=[whole_vmem()] * 4 + [pl.BlockSpec(memory_space=pl.ANY)] * 2,
            out_specs=(pl.BlockSpec(memory_space=pl.ANY), whole_vmem()),
            scratch_shapes=[
                pltpu.VMEM((boards, padded, padded), BF16),
                pltpu.SMEM(slots.shape, jnp.int32),
                pltpu.VMEM((CORES * rivers * held_rows, LANES), F32),
                pltpu.VMEM((padded, LANES), F32),
                pltpu.VMEM((boards, LANES // blocks, padded), BF16),
                pltpu.VMEM((boards * LANES // blocks, padded), BF16),
                pltpu.VMEM((boards, entries, hands), F32),
                pltpu.SemaphoreType.DMA((boards,)),
                pltpu.SemaphoreType.DMA(()),
                pltpu.SemaphoreType.DMA((boards,)),
            ],
            compiler_params=pltpu.CompilerParams(vmem_limit_bytes=40 * 2**20),
        )(mine, other, hand_rows, cards, contest, slots)
    with jax.named_scope("means"):
        by_river = lax.all_to_all(partial, "river", split_axis=0, concat_axis=0, tiled=True)
        turn_value, partial = pl.pallas_call(
            functools.partial(river_mean_kernel, 1.0 / (rivers * rivers_here)),
            out_shape=(
                jax.ShapeDtypeStruct((entries, hands), F32),
                jax.ShapeDtypeStruct((turns, entries, padded), I16),
            ),
            in_specs=[whole_vmem()],
            out_specs=(whole_vmem(), whole_vmem()),
            compiler_params=pltpu.CompilerParams(vmem_limit_bytes=SMALL),
        )(by_river)
        by_turn = lax.all_to_all(partial, "turn", split_axis=0, concat_axis=0, tiled=True)
        turn_value, flop_value = pl.pallas_call(
            functools.partial(turn_mean_kernel, 1.0 / (turns * turns_here)),
            out_shape=(
                jax.ShapeDtypeStruct(turn_value.shape, F32),
                jax.ShapeDtypeStruct((entries, hands), F32),
            ),
            in_specs=[whole_vmem()] * 2,
            out_specs=(whole_vmem(), whole_vmem()),
            compiler_params=pltpu.CompilerParams(vmem_limit_bytes=SMALL),
        )(by_turn, turn_value)
    river_value = river.reshape(turns_here, rivers_here, entries, hands)
    return river_value, turn_value[None], flop_value


def solution(mesh):
    return jax.shard_map(
        local,
        mesh=mesh,
        in_specs=(
            P("turn", "river", None),
            P("turn", "river", None),
            P("turn", "river", None),
            P("turn", "river", None),
            P(("river", "bucket"), None),
            P("bucket", None),
            P("bucket"),
            P("bucket"),
        ),
        out_specs=(
            P("turn", "river", "bucket", None),
            P("turn", "bucket", None),
            P("bucket", None),
        ),
        check_vma=False,
    )
```

```python
import functools

import jax
import jax.numpy as jnp
import numpy as np
from jax import lax
from jax.experimental import pallas as pl
from jax.experimental.pallas import tpu as pltpu
from jax.sharding import PartitionSpec as P

OPTIONS = 2
REPLIES = 8
LANES = 128
CARDS = 52
TILE = 16
CORES = 2
CONTEST_PLACES = 16
SMALL = 8 * 2**20
F32 = jnp.float32
BF16 = jnp.bfloat16
I16 = jnp.int16
POT_MOST = 24.0
POT_LEAST = 2.0
CHANCE_LEAST = 0.049804688
CODE_MOST = 32000.0


def card_table(count, padded):
    table = np.zeros((LANES, padded), np.float32)
    for cards in np.triu_indices(CARDS, 1):
        table[cards[:count], np.arange(count)] = 1.0
    return jnp.asarray(table, BF16)


def code_scale(floor, most):
    return CODE_MOST / np.log2(1.0 + most / floor)


def sum_code(hands, depth):
    most = REPLIES * POT_MOST / hands
    floor = POT_LEAST / hands * CHANCE_LEAST**depth
    return floor, code_scale(floor, most)


def dither(rows, river):
    row = lax.broadcasted_iota(jnp.int32, (rows, LANES), 0)
    lane = lax.broadcasted_iota(jnp.int32, (rows, LANES), 1)
    place = (row * 3091 + lane * 2333 + river * 1697) & 4095
    return (place.astype(F32) + 0.5) * (1.0 / 4096)


def encode(x, offset, floor, scale):
    size = jnp.log(1.0 + jnp.abs(x) * (1.0 / floor)) * (scale / np.log(2.0))
    size = jnp.minimum(jnp.floor(size + offset), 32767.0)
    return jnp.where(x < 0, -size, size).astype(jnp.int32).astype(I16)


def decode(code, offset, floor, scale):
    code = code.astype(jnp.int32).astype(F32)
    size = (jnp.abs(code) + (0.5 - offset)) * (np.log(2.0) / scale)
    size = (jnp.exp(size) - 1.0) * floor
    return jnp.where(code == 0, 0.0, jnp.where(code < 0, -size, size))


def encode_rows(x, hands):
    most = jnp.maximum(jnp.max(jnp.abs(x), axis=1, keepdims=True), 1e-30)
    power = jnp.floor(jnp.log(most) * (1.0 / np.log(2.0)) + 1.0)
    code = jnp.floor(x * (jnp.exp(power * -np.log(2.0)) * CODE_MOST) + 0.5)
    lane = lax.broadcasted_iota(jnp.int32, x.shape, 1)
    return jnp.where(lane == hands, power, code).astype(jnp.int32).astype(I16)


def sum_decoded(codes_ref, hands):
    total = None
    for index in range(codes_ref.shape[0]):
        code = codes_ref[index].astype(jnp.int32).astype(F32)
        step = jnp.exp(code[:, hands : hands + 1] * np.log(2.0)) * (1.0 / CODE_MOST)
        part = code * step
        total = part if total is None else total + part
    return total


def split_two(x):
    high = x.astype(BF16)
    return high, (x - high.astype(F32)).astype(BF16)


def split_three(x):
    high = x.astype(BF16)
    rest = x - high.astype(F32)
    middle = rest.astype(BF16)
    return high, middle, (rest - middle.astype(F32)).astype(BF16)


def dot_rows(a, b):
    return lax.dot_general(a, b, (((1,), (1,)), ((), ())), preferred_element_type=F32)


def line_sum_kernel(hand_count, code, rows_ref, info_ref, sums_ref):
    blocks, rows, width = rows_ref.shape
    depth, lines = info_ref.shape
    depth -= 2
    entries = lines // (OPTIONS * REPLIES)
    table = [rows_ref[block].astype(F32) for block in range(blocks)]
    table = jnp.concatenate(table, axis=0).astype(BF16)
    column = lax.broadcasted_iota(jnp.int32, (width, lines), 0).astype(F32)
    picks = [
        (column == info_ref[step : step + 1, :]).astype(F32).astype(BF16) for step in range(depth)
    ]
    picks = jnp.concatenate(picks, axis=1)
    present = jnp.dot(jnp.ones((8, width), BF16), picks, preferred_element_type=F32)
    looked = jnp.dot(table, picks, preferred_element_type=F32) + (1.0 - present[0:1])
    product = looked[:, 0:lines]
    for step in range(1, depth):
        product = product * looked[:, step * lines : (step + 1) * lines]
    kind = info_ref[depth : depth + 1, :]
    scale = info_ref[depth + 1 : depth + 2, :] / hand_count
    sign = jnp.where(kind == 1.0, 1.0, jnp.where(kind == 2.0, -1.0, 0.0))
    weights = (jnp.where(kind == 0.0, scale, 0.0), sign * scale)
    line = lax.broadcasted_iota(jnp.int32, (lines, LANES), 0)
    lane = lax.broadcasted_iota(jnp.int32, (lines, LANES), 1)
    slot = ((line // REPLIES) % OPTIONS) * entries + line // (REPLIES * OPTIONS)
    group = OPTIONS * entries
    terms, targets = [], []
    for kind_index, weight in enumerate(weights):
        terms.extend(split_three(product * weight))
        targets.extend([(lane == slot + kind_index * group).astype(F32).astype(BF16)] * 3)
    summed = jnp.dot(
        jnp.concatenate(terms, axis=1),
        jnp.concatenate(targets, axis=0),
        preferred_element_type=F32,
    )
    total = summed[0:rows]
    for block in range(1, blocks):
        part = summed[block * rows : (block + 1) * rows]
        total += pltpu.roll(part, block * 2 * group, 1)
    codes = encode(total, dither(rows, lax.axis_index("river")), *code)
    for copy in range(sums_ref.shape[0]):
        sums_ref[copy] = codes


def prepare_kernel(
    shard_rows, held_rows, blocks, rivers, reach_hbm, live_hbm, rank_hbm, bucket_hbm,
    cards_hbm, contest_hbm, rows_ref, slots_ref, token_ref, cards_ref, reach_ref, live_ref, rank_ref,
    bucket_ref, index_ref, turned_ref, contest_ref, in_sems, sems,
):
    arrays = (reach_hbm, live_hbm, rank_hbm, bucket_hbm, cards_hbm)
    places = (reach_ref, live_ref, rank_ref, bucket_ref, cards_ref)
    copies = []
    for index, (array, place) in enumerate(zip(arrays, places)):
        copies.append(pltpu.make_async_copy(array, place, in_sems.at[index]))
        copies[-1].start()
    boards, hands = reach_ref.shape
    padded = cards_ref.shape[1]
    chunks = padded // LANES
    token_ref[...] = jnp.zeros(token_ref.shape, I16)
    for copy in copies:
        copy.wait()
    bucket = bucket_ref[...].astype(F32)
    owner = jnp.floor((bucket + 0.5) * (1.0 / shard_rows))
    row = bucket - owner * shard_rows
    place = jnp.floor((owner + 0.5) * (1.0 / blocks))
    half = jnp.where(row >= held_rows, 1.0, 0.0)
    row = row - half * (shard_rows - held_rows)
    core = lax.rem(lax.axis_index("turn"), CORES).astype(F32)
    elsewhere = jnp.where(half == core, 0.0, 1.0)
    index_ref[...] = jnp.zeros(index_ref.shape, F32)
    index_ref[:, 0:hands] = (elsewhere * rivers + place) * held_rows + row
    slots_ref[...] = jnp.zeros(slots_ref.shape, jnp.int32)
    for board in range(boards):
        for chunk in range(chunks):
            slot = index_ref[board : board + 1, chunk * LANES : (chunk + 1) * LANES]
            at = board * chunks + chunk
            slots_ref[at : at + 1, :] = slot.astype(jnp.int32)
    rows_ref[...] = jnp.zeros(rows_ref.shape, F32)
    rows_ref[0:boards, 0:hands] = owner - place * blocks
    live = live_ref[...].astype(F32)
    rows_ref[boards : 2 * boards, 0:hands] = reach_ref[...] * live
    rows_ref[2 * boards : 3 * boards, 0:hands] = live

    turned_ref[...] = jnp.zeros(turned_ref.shape, F32)
    turned_ref[0:boards, 0:hands] = rank_ref[...].astype(F32)
    rank_rows = turned_ref[0:8, :]
    copies = []
    for chunk in range(chunks):
        lines = pl.ds(chunk * LANES, LANES)
        ranks = turned_ref[:, lines].T
        cards = cards_ref[:, lines].astype(F32).T.astype(BF16)
        shared = jnp.dot(cards, cards_ref[...], preferred_element_type=F32)
        for board in range(boards):
            order = rank_rows[board : board + 1, :] - ranks[:, board : board + 1]
            contest = jnp.where(shared == 0.0, jnp.clip(order, -1.0, 1.0), 0.0)
            contest_ref[board, lines, :] = contest.astype(jnp.int32).astype(jnp.int8)
        copy = pltpu.make_async_copy(
            contest_ref.at[:, lines, :], contest_hbm.at[0:boards, lines, :], sems.at[chunk]
        )
        copy.start()
        copies.append(copy)
    around = cards_ref[TILE * (CARDS // TILE) : TILE * (CARDS // TILE + 1), :].astype(F32)
    row = lax.broadcasted_iota(jnp.int32, around.shape, 0)
    around = jnp.where(row == CARDS % TILE, 1.0, around).astype(BF16)
    cards_ref[TILE * (CARDS // TILE) : TILE * (CARDS // TILE + 1), :] = around
    for copy in copies:
        copy.wait()


def board_kernel(
    blocks, in_code, mine_ref, other_ref, rows_ref, cards_ref, contest_hbm, slots_hbm, river_hbm,
    part_ref, contest_ref, slots_ref, plain_ref, found_ref, show_ref, fold_ref, river_ref,
    contest_sems, slots_sem, river_sems,
):
    boards, _, hands = river_ref.shape
    padded = cards_ref.shape[1]
    chunks = padded // LANES
    rivers, held_rows, _ = mine_ref.shape
    columns = LANES // blocks
    half = columns // 2
    entries = half // OPTIONS
    slots_copy = pltpu.make_async_copy(slots_hbm, slots_ref, slots_sem)
    slots_copy.start()
    contest_copies = []
    for board in range(boards):
        contest_copies.append(
            pltpu.make_async_copy(
                contest_hbm.at[board], contest_ref.at[board], contest_sems.at[board]
            )
        )
        contest_copies[board].start()

    for river in range(rivers):
        offset = dither(held_rows, river)
        for part, ref in enumerate((mine_ref, other_ref)):
            at = (part * rivers + river) * held_rows
            plain_ref[at : at + held_rows, :] = decode(ref[river], offset, *in_code)
    slots_copy.wait()

    def place(board, chunk):
        lanes = pl.ds(pl.multiple_of(chunk * LANES, LANES), LANES)
        found = found_ref[lanes, :].T
        group = rows_ref[board : board + 1, lanes]
        reach = rows_ref[boards + board : boards + board + 1, lanes]
        chosen = jnp.zeros((columns, LANES), F32)
        for which in range(blocks):
            chosen += jnp.where(
                group == which, found[which * columns : (which + 1) * columns], 0.0
            )
        high, low = split_two(chosen * reach)
        show_ref[board, 0:half, lanes] = high[0:half]
        show_ref[board, half:columns, lanes] = low[0:half]
        base = board * half
        fold_ref[base : base + half, lanes] = high[half:columns]
        base = (boards + board) * half
        fold_ref[base : base + half, lanes] = low[half:columns]

    def find(board, chunk):
        base = pl.multiple_of(chunk * LANES, LANES)
        for hand in range(LANES):
            slot = slots_ref[board * chunks + chunk, hand]
            found_ref[pl.ds(base + hand, 1), :] = plain_ref[pl.ds(slot, 1), :]

    for board in range(boards):
        find(board, 0)

        def gather(chunk, carry, board=board):
            place(board, chunk - 1)
            find(board, chunk)
            return carry

        lax.fori_loop(1, chunks, gather, 0)
        place(board, chunks - 1)

    cards = cards_ref[...]
    folds = fold_ref[...]
    held_by = dot_rows(folds, cards)
    held_by = held_by[0 : boards * half] + held_by[boards * half : 2 * boards * half]
    lane = lax.broadcasted_iota(jnp.int32, held_by.shape, 1)
    held_by = jnp.where(lane == CARDS, held_by, -held_by)
    spread = jnp.dot(
        jnp.concatenate(split_three(held_by), axis=0), cards, preferred_element_type=F32
    )
    folded = folds[0 : boards * half].astype(F32) + folds[boards * half :].astype(F32)
    for piece in range(3):
        folded += spread[piece * boards * half : (piece + 1) * boards * half]
    total = None
    river_copies = []
    for board in range(boards):
        contest_copies[board].wait()
        shown = jnp.dot(
            show_ref[board], contest_ref[board].astype(BF16), preferred_element_type=F32
        )
        value = shown[0:half] + shown[half:columns] + folded[board * half : (board + 1) * half]
        best = jnp.maximum(value[0:entries], value[entries:half])
        best = best * rows_ref[2 * boards + board : 2 * boards + board + 1, :]
        river_ref[board] = best[:, 0:hands]
        river_copies.append(
            pltpu.make_async_copy(river_ref.at[board], river_hbm.at[board], river_sems.at[board])
        )
        river_copies[board].start()
        total = best if total is None else total + best
    codes = encode_rows(total, hands)
    for copy in range(part_ref.shape[0]):
        part_ref[copy] = codes
    for copy in river_copies:
        copy.wait()


def river_mean_kernel(share, codes_ref, mean_ref, part_ref):
    hands = mean_ref.shape[1]
    mean = sum_decoded(codes_ref, hands) * share
    mean_ref[...] = mean[:, 0:hands]
    lane = lax.broadcasted_iota(jnp.int32, mean.shape, 1)
    codes = encode_rows(jnp.where(lane < hands, mean, 0.0), hands)
    for copy in range(part_ref.shape[0]):
        part_ref[copy] = codes


def turn_mean_kernel(share, codes_ref, turn_ref, turn_out_ref, mean_ref):
    hands = mean_ref.shape[1]
    turn_out_ref[...] = turn_ref[...]
    mean_ref[...] = sum_decoded(codes_ref, hands)[:, 0:hands] * share


def follow_kernel(value_ref, token_ref, out_ref):
    del value_ref, token_ref, out_ref


def whole_vmem():
    return pl.BlockSpec(memory_space=pltpu.VMEM)


def local(reach_in, hand_live, hand_rank, hand_bucket, strategy, line_acts, line_kind, line_pot):
    turns_here, rivers_here, hands = reach_in.shape
    boards = turns_here * rivers_here
    shard_rows, width = strategy.shape
    lines = line_acts.shape[0]
    entries = lines // (OPTIONS * REPLIES)
    blocks = lax.axis_size("bucket")
    rivers = lax.axis_size("river")
    turns = lax.axis_size("turn")
    padded = -(-hands // LANES) * LANES
    held_rows = -(-shard_rows // (CORES * 8)) * 8
    core = lax.axis_index("turn") % CORES

    with jax.named_scope("share_rows"):
        first = core * (shard_rows - held_rows)
        part = lax.dynamic_slice_in_dim(strategy, first, held_rows, axis=0)
        rows = lax.all_to_all(
            jnp.broadcast_to(part[None], (blocks, held_rows, width)),
            "bucket",
            split_axis=0,
            concat_axis=0,
            tiled=True,
        )
    in_code = sum_code(hands, line_acts.shape[1])
    info = [line_acts.T.astype(F32), line_kind.astype(F32)[None], line_pot[None]]
    info = jnp.concatenate(info, axis=0)
    with jax.named_scope("line_sums"):
        sums = pl.pallas_call(
            functools.partial(line_sum_kernel, hands, in_code),
            out_shape=jax.ShapeDtypeStruct((rivers, held_rows, LANES), I16),
            in_specs=[whole_vmem()] * 2,
            out_specs=whole_vmem(),
            compiler_params=pltpu.CompilerParams(vmem_limit_bytes=16 * 2**20),
        )(rows, info)
    cards = card_table(hands, padded)
    live = hand_live.reshape(boards, hands)
    with jax.named_scope("share_sums"):
        mine = lax.all_to_all(sums, "river", split_axis=0, concat_axis=0, tiled=True)
    with jax.named_scope("prepare"):
        chunks = padded // LANES
        slot_shape = (-(-boards * chunks // 8) * 8, LANES)
        contest, hand_rows, slots, token, cards = pl.pallas_call(
            functools.partial(prepare_kernel, shard_rows, held_rows, blocks, rivers),
            out_shape=(
                jax.ShapeDtypeStruct((CONTEST_PLACES, padded, padded), jnp.int8),
                jax.ShapeDtypeStruct((8, padded), F32),
                jax.ShapeDtypeStruct(slot_shape, jnp.int32),
                jax.ShapeDtypeStruct((16, LANES), I16),
                jax.ShapeDtypeStruct(cards.shape, BF16),
            ),
            in_specs=[pl.BlockSpec(memory_space=pl.ANY)] * 5,
            out_specs=(pl.BlockSpec(memory_space=pl.ANY),) + (whole_vmem(),) * 4,
            scratch_shapes=[
                pltpu.VMEM((boards, hands), F32),
                pltpu.VMEM((boards, hands), jnp.int32),
                pltpu.VMEM((boards, hands), jnp.int32),
                pltpu.VMEM((boards, hands), jnp.int32),
                pltpu.VMEM((boards, padded), F32),
                pltpu.VMEM((LANES, padded), F32),
                pltpu.VMEM((boards, padded, padded), jnp.int8),
                pltpu.SemaphoreType.DMA((5,)),
                pltpu.SemaphoreType.DMA((chunks,)),
            ],
            cost_estimate=pl.CostEstimate(
                flops=8 * boards * padded * padded,
                bytes_accessed=(boards + 1) * 2 * padded * padded,
                transcendentals=0,
            ),
            compiler_params=pltpu.CompilerParams(vmem_limit_bytes=40 * 2**20),
        )(
            reach_in.reshape(boards, hands),
            live,
            hand_rank.reshape(boards, hands),
            hand_bucket.reshape(boards, hands),
            cards,
        )
    with jax.named_scope("share_sums"):
        mine = pl.pallas_call(
            follow_kernel,
            out_shape=jax.ShapeDtypeStruct(mine.shape, mine.dtype),
            in_specs=[whole_vmem()] * 2,
            out_specs=whole_vmem(),
            input_output_aliases={0: 0},
            compiler_params=pltpu.CompilerParams(vmem_limit_bytes=SMALL),
        )(mine, token)
        swap = [(device, device ^ 1) for device in range(turns)]
        other = lax.ppermute(mine, "turn", swap)
    with jax.named_scope("boards"):
        river, partial = pl.pallas_call(
            functools.partial(board_kernel, blocks, in_code),
            out_shape=(
                jax.ShapeDtypeStruct((boards, entries, hands), F32),
                jax.ShapeDtypeStruct((rivers, entries, padded), I16),
            ),
            in_specs=[whole_vmem()] * 4 + [pl.BlockSpec(memory_space=pl.ANY)] * 2,
            out_specs=(pl.BlockSpec(memory_space=pl.ANY), whole_vmem()),
            scratch_shapes=[
                pltpu.VMEM((boards, padded, padded), jnp.int8),
                pltpu.SMEM(slots.shape, jnp.int32),
                pltpu.VMEM((CORES * rivers * held_rows, LANES), F32),
                pltpu.VMEM((padded, LANES), F32),
                pltpu.VMEM((boards, LANES // blocks, padded), BF16),
                pltpu.VMEM((boards * LANES // blocks, padded), BF16),
                pltpu.VMEM((boards, entries, hands), F32),
                pltpu.SemaphoreType.DMA((boards,)),
                pltpu.SemaphoreType.DMA(()),
                pltpu.SemaphoreType.DMA((boards,)),
            ],
            compiler_params=pltpu.CompilerParams(vmem_limit_bytes=40 * 2**20),
        )(mine, other, hand_rows, cards, contest, slots)
    with jax.named_scope("means"):
        by_river = lax.all_to_all(partial, "river", split_axis=0, concat_axis=0, tiled=True)
        turn_value, partial = pl.pallas_call(
            functools.partial(river_mean_kernel, 1.0 / (rivers * rivers_here)),
            out_shape=(
                jax.ShapeDtypeStruct((entries, hands), F32),
                jax.ShapeDtypeStruct((turns, entries, padded), I16),
            ),
            in_specs=[whole_vmem()],
            out_specs=(whole_vmem(), whole_vmem()),
            compiler_params=pltpu.CompilerParams(vmem_limit_bytes=SMALL),
        )(by_river)
        by_turn = lax.all_to_all(partial, "turn", split_axis=0, concat_axis=0, tiled=True)
        turn_value, flop_value = pl.pallas_call(
            functools.partial(turn_mean_kernel, 1.0 / (turns * turns_here)),
            out_shape=(
                jax.ShapeDtypeStruct(turn_value.shape, F32),
                jax.ShapeDtypeStruct((entries, hands), F32),
            ),
            in_specs=[whole_vmem()] * 2,
            out_specs=(whole_vmem(), whole_vmem()),
            compiler_params=pltpu.CompilerParams(vmem_limit_bytes=SMALL),
        )(by_turn, turn_value)
    river_value = river.reshape(turns_here, rivers_here, entries, hands)
    return river_value, turn_value[None], flop_value


def solution(mesh):
    return jax.shard_map(
        local,
        mesh=mesh,
        in_specs=(
            P("turn", "river", None),
            P("turn", "river", None),
            P("turn", "river", None),
            P("turn", "river", None),
            P(("river", "bucket"), None),
            P("bucket", None),
            P("bucket"),
            P("bucket"),
        ),
        out_specs=(
            P("turn", "river", "bucket", None),
            P("turn", "bucket", None),
            P("bucket", None),
        ),
        check_vma=False,
    )
```
